1024 devices in a mesh: blk: 64 (over z, x), pair: 16 (over y, core).
Axes of the slice: x: 8, y: 8, z: 8, core: 2. Of those that a mesh axis runs over, the one named last changes fastest.
Arguments:
- centroids: float32 [3, 65536], P(None, 'blk'), may hold values from -6 to 6
- normals: float32 [3, 65536], P(None, 'blk'), may hold values from -4 to 4
- areas: float32 [65536], P('blk'), may hold values from 0.3 to 3
- cotangent: float32 [], replicated, may hold values from 6.1035156e-05 to 0.00024414062
- pair_code: int32 [64, 16, 64, 1], P('blk', 'pair'), may hold values from -1 to 15, as said below
- corner_vertex: int32 [3, 73728], P(None, 'blk'), may hold values from -1 to 511, as said below
Outputs:
- vertex_grad: float32 [3, 32768], P(None, 'blk')
- face_grad: float32 [4, 65536], P(None, 'blk')
The draws below stay inside these ranges and needn't reach their ends.
Inputs may be any that keep to these rules, and one draw needn't show every extreme that they name: `pair_code`: an entry other than -1 at (q, p, b, c) is t * 4 + s with target block t of blk index b and source block s of blk index q, never the same block. `corner_vertex`: every corner of every face is named by exactly one entry other than -1 over all windows, in the window of the blk index that owns its vertex.
All inputs are finite; a program needn't handle non-finite values.
Results may differ from the reference program's by a relative error of at most 0.0003.
Values sent between devices are 32-bit elements; how exact they have to be, the bound alone decides.
No kernel may reach another device: no remote copies, remote signals or barrier semaphores. Data moves between devices by JAX's collectives and lax.ppermute only.
A program may use at most 32 MiB of HBM per device.

```python
import math
import jax
import jax.numpy as jnp
from jax import lax

BLOCK = 256
FB_DEV = 4
CAP = 1
HALO_FACES = 64
FACES_DEV = 1024
FACES = 65536
VERTS_DEV = 512
VERTS = 32768
WINDOW = 1152
N_BLK = 64
N_PAIR = 16


def draw_pair_code(key, part):
    key_spread, key_ticket, key_target, key_source = jax.random.split(key, 4)
    spread = jax.random.randint(key_spread, (N_PAIR, N_BLK), 300, 900)
    thresh = spread * spread // 1000
    shape = (N_BLK, N_PAIR, N_BLK, CAP)
    ticket = jax.random.randint(key_ticket, shape, 0, 1000)
    active = ticket < thresh[None, :, :, None]
    target = jax.random.randint(key_target, shape, 0, FB_DEV)
    source = jax.random.randint(key_source, shape, 0, FB_DEV)
    sender = jnp.arange(N_BLK, dtype=jnp.int32)[:, None, None, None]
    receiver = jnp.arange(N_BLK, dtype=jnp.int32)[None, None, :, None]
    clash = jnp.logical_and(sender == receiver, source == target)
    source = jnp.where(clash, (target + 1) % FB_DEV, source)
    return jnp.where(active, target * FB_DEV + source, -1).astype(jnp.int32)


def draw_corner_vertex(key, part):
    reach = HALO_FACES // 2
    offset = jax.random.randint(key, (3, FACES), -reach, reach + 1)
    device = jnp.arange(N_BLK, dtype=jnp.int32)[:, None]
    place = jnp.arange(WINDOW, dtype=jnp.int32)[None, :]
    face_index = (device * FACES_DEV + place - HALO_FACES) % FACES
    vertex = (face_index[None] // 2 + offset[:, face_index]) % VERTS
    holder = vertex // VERTS_DEV
    local_vertex = jnp.where(holder == device[None], vertex - device[None] * VERTS_DEV, -1)
    return local_vertex.reshape(3, N_BLK * WINDOW).astype(jnp.int32)


def block_levels(key, shape, cuts, least, largest):
    loudness, own = 1.0, jax.random.fold_in(key, 6)
    for axis_at, blocks in cuts:
        draws = jnp.exp(jax.random.uniform(jax.random.fold_in(own, axis_at), (blocks,), jnp.float32, least / len(cuts), largest / len(cuts)))
        loudness = loudness * jnp.repeat(draws, shape[axis_at] // blocks).reshape([-1 if axis == axis_at else 1 for axis in range(len(shape))])
    return loudness


def noise(own_key, dims, scale, limit, pieces=(), kind=jnp.bfloat16):
    loudness = block_levels(own_key, dims, pieces, -0.22, 0.18) if pieces else 1.0
    array = jax.random.normal(own_key, dims, jnp.float32) * scale * loudness
    return jnp.minimum(jnp.maximum(array, -limit), limit).astype(kind)


def setup_inputs(seed: int = 0) -> dict:
    key_of = jax.random.split(jax.random.key(seed), 7)
    return {
        "centroids": noise(key_of[0], (3, FACES), 1.0, 6.0, ((1, 64),), jnp.float32),
        "normals": noise(key_of[1], (3, FACES), 0.6, 4.0, ((1, 64),), jnp.float32),
        "areas": jnp.clip(jnp.exp(math.log(3.0) - 2.3025851 * jax.random.uniform(key_of[2], (FACES,), jnp.float32) ** block_levels(key_of[2], (FACES,), ((0, 64),), -0.2, 0.2)), 0.3, 3.0),
        "cotangent": jnp.clip(jax.random.uniform(key_of[3], (), jnp.float32, 6.103515625e-05, 0.00024414062), 6.103515625e-05, 0.00024414062),
        "pair_code": draw_pair_code(jax.random.fold_in(key_of[6], 71), 0),
        "corner_vertex": draw_corner_vertex(jax.random.fold_in(key_of[6], 71), 0),
    }


soften = 1.0
tile_group = 4


def pair_terms(center_blocks, normal_blocks, area_blocks, sources, targets, cotangent):
    slot_count = targets.shape[0]
    block_width = center_blocks.shape[2]
    blocks = center_blocks.shape[1]
    active = targets >= 0
    active_count = jnp.sum(active.astype(jnp.int32)).astype(jnp.int32)
    ordering = jnp.argsort(jnp.where(active, 0, 1).astype(jnp.int32), stable=True).astype(jnp.int32)
    rounds = ((active_count + tile_group - 1) // tile_group).astype(jnp.int32)
    target_init = jnp.zeros((7, blocks, block_width), jnp.float32)
    source_init = jnp.zeros((4, slot_count, block_width), jnp.float32)

    def one_round(round_index, totals):
        target_sum, source_sum = totals
        picked = lax.dynamic_slice_in_dim(ordering, (round_index * tile_group).astype(jnp.int32), tile_group)
        chosen = targets[picked]
        weight_on = (chosen >= 0).astype(jnp.float32)
        target_block = jnp.maximum(chosen, 0).astype(jnp.int32)
        source_rows = sources[:, picked]
        target_center = center_blocks[:, target_block]
        target_normal = normal_blocks[:, target_block]
        target_area = area_blocks[target_block]
        offsets = target_center[:, :, :, None] - source_rows[0:3, :, None, :]
        projected = jnp.sum(target_normal[:, :, :, None] * offsets, axis=0)
        distance = jnp.sum(offsets * offsets, axis=0) + soften
        numerator = projected * projected + soften
        inverse = 1.0 / (distance * distance)
        kernel = numerator * inverse
        weight = cotangent * weight_on[:, None, None] * target_area[:, :, None] * source_rows[3][:, None, :]
        pulling = 2.0 * weight * projected * inverse
        pushing = 4.0 * weight * numerator * inverse / distance
        forces = pulling[None] * target_normal[:, :, :, None] - pushing[None] * offsets
        energy_rate = cotangent * weight_on[:, None, None] * kernel
        target_part = jnp.concatenate([
            jnp.sum(forces, axis=-1),
            jnp.sum(pulling[None] * offsets, axis=-1),
            jnp.sum(energy_rate * source_rows[3][:, None, :], axis=-1)[None]], axis=0)
        source_part = jnp.concatenate([
            -jnp.sum(forces, axis=-2),
            jnp.sum(energy_rate * target_area[:, :, None], axis=-2)[None]], axis=0)
        pick_table = (target_block[:, None] == jnp.arange(blocks, dtype=jnp.int32)[None, :]).astype(jnp.float32) * weight_on[:, None]
        target_sum = target_sum + jnp.einsum("gf,kgb->kfb", pick_table, target_part, precision=lax.Precision.HIGHEST)
        source_sum = source_sum.at[:, picked].add(source_part)
        return target_sum, source_sum

    return lax.fori_loop(jnp.int32(0), rounds, one_round, (target_init, source_init))


def reference(centroids, normals, areas, cotangent, pair_code, corner_vertex):
    blocks = FB_DEV
    block_total = N_BLK * FB_DEV
    center_blocks = centroids.reshape(3, block_total, BLOCK)
    normal_blocks = normals.reshape(3, block_total, BLOCK)
    area_blocks = areas.reshape(block_total, BLOCK)
    owner = jnp.arange(N_BLK, dtype=jnp.int32)[:, None]

    def receive(face_sum, index):
        receiver = (index // N_PAIR).astype(jnp.int32)
        member = (index % N_PAIR).astype(jnp.int32)
        plane = lax.dynamic_index_in_dim(pair_code, member, 1, keepdims=False)
        incoming = lax.dynamic_index_in_dim(plane, receiver, 1, keepdims=False)
        live_in = incoming >= 0
        global_block = (owner * blocks + jnp.where(live_in, incoming % blocks, 0)).reshape(-1).astype(jnp.int32)
        targets = jnp.where(live_in, incoming // blocks, -1).reshape(-1).astype(jnp.int32)
        source_rows = jnp.concatenate([center_blocks[:, global_block], area_blocks[global_block][None]], axis=0)
        start = (receiver * blocks).astype(jnp.int32)
        local_center = lax.dynamic_slice_in_dim(center_blocks, start, blocks, axis=1)
        local_normal = lax.dynamic_slice_in_dim(normal_blocks, start, blocks, axis=1)
        local_area = lax.dynamic_slice_in_dim(area_blocks, start, blocks, axis=0)
        target_sum, source_sum = pair_terms(local_center, local_normal, local_area, source_rows, targets, cotangent)
        own_index = (start + jnp.arange(blocks, dtype=jnp.int32)).astype(jnp.int32)
        face_sum = face_sum.at[:, own_index].add(target_sum)
        face_sum = face_sum.at[0:3, global_block].add(source_sum[0:3])
        face_sum = face_sum.at[6, global_block].add(source_sum[3])
        return face_sum, None

    face_sum, ignored = lax.scan(receive, jnp.zeros((7, block_total, BLOCK), jnp.float32),
                                 jnp.arange(N_BLK * N_PAIR, dtype=jnp.int32))
    flat = face_sum.reshape(7, FACES)
    center_grad = flat[0:3]

    def vertex_part(device):
        place = ((device * FACES_DEV + jnp.arange(WINDOW, dtype=jnp.int32) - HALO_FACES) % FACES).astype(jnp.int32)
        extended = center_grad[:, place]
        table = lax.dynamic_slice_in_dim(corner_vertex, (device * WINDOW).astype(jnp.int32), WINDOW, axis=1)
        columns = jnp.arange(VERTS_DEV, dtype=jnp.int32)[None, :]
        incidence = ((table[0][:, None] == columns).astype(jnp.float32)
                     + (table[1][:, None] == columns).astype(jnp.float32)
                     + (table[2][:, None] == columns).astype(jnp.float32))
        return jnp.dot(extended, incidence, precision=lax.Precision.HIGHEST) / 3.0

    vertex_parts = lax.map(vertex_part, jnp.arange(N_BLK, dtype=jnp.int32))
    vertex_grad = jnp.transpose(vertex_parts, (1, 0, 2)).reshape(3, VERTS)
    return vertex_grad, flat[3:7]
```

```python
import functools

import jax
import jax.numpy as jnp
from jax import lax
from jax.experimental import pallas as pl
from jax.experimental.pallas import tpu as pltpu
from jax.sharding import PartitionSpec as P

BLOCK = 256
FB_DEV = 4
HALO_FACES = 64
CODES = FB_DEV * FB_DEV
ROWS = 32
F32 = jnp.float32
VMEM = pl.BlockSpec(memory_space=pltpu.VMEM)
SMEM = pl.BlockSpec(memory_space=pltpu.SMEM)


def fold(values):
    return jnp.sum(values.reshape(ROWS // 8, 8, BLOCK), axis=0)


def reciprocal(values):
    guess = pl.reciprocal(values, approx=True)
    return guess * (2.0 - values * guess)


def cell(own, partner_ref, block, count, as_target):
    def step(at, totals):
        rows = partner_ref[block, pl.ds(pl.multiple_of(at * ROWS, ROWS), ROWS), :]
        column = [rows[:, c : c + 1] for c in range(7)]
        offset = [own[c] - column[c] for c in range(3)]
        normal = own[3:6] if as_target else column[3:6]
        projected = normal[0] * offset[0] + normal[1] * offset[1] + normal[2] * offset[2]
        distance = offset[0] * offset[0] + offset[1] * offset[1] + (offset[2] * offset[2] + 1.0)
        inverse = reciprocal(distance)
        weight = inverse * inverse * (column[6] * count)
        kernel = (projected * projected + 1.0) * weight
        pulling = projected * weight
        pushing = kernel * inverse
        terms = [kernel] + [pushing * offset[c] for c in range(3)]
        if as_target:
            terms += [pulling] + [pulling * offset[c] for c in range(3)]
        else:
            terms += [pulling * normal[c] for c in range(3)]
        return tuple(t + fold(v) for t, v in zip(totals, terms))

    zero = jnp.zeros((8, BLOCK), F32)
    return lax.fori_loop(0, BLOCK // ROWS, step, (zero,) * (8 if as_target else 7), unroll=2)


def pair_kernel(as_target, own_blocks, group, codes_ref, scale_ref, own_ref, *refs):
    partners, (base_ref, out_ref, cols_ref, acc_ref, count_ref) = refs[:group], refs[group:]
    shares = codes_ref.shape[1]
    slots = group * CODES

    def clear(i, carry):
        count_ref[i] = 0
        return carry

    lax.fori_loop(0, slots, clear, 0)

    def tally(i, carry):
        code = codes_ref[i // shares, i % shares]

        @pl.when(code >= 0)
        def _():
            at = (i // shares) * CODES + code
            count_ref[at] = count_ref[at] + 1

        return carry

    lax.fori_loop(0, group * shares, tally, 0)

    for k in range(group):
        for s in range(FB_DEV):
            cols_ref[k * FB_DEV + s, :, 0:8] = partners[k][:, s * BLOCK : (s + 1) * BLOCK].T
    acc_ref[...] = jnp.zeros_like(acc_ref)

    def visit(i, carry):
        count = count_ref[i]
        code = i % CODES
        first, second = code // FB_DEV, code % FB_DEV
        mine, other = (first, second) if as_target else (second, first)
        wanted = count > 0
        if len(own_blocks) < FB_DEV:
            wanted = jnp.logical_and(wanted, functools.reduce(jnp.logical_or, [mine == o for o in own_blocks]))

        @pl.when(wanted)
        def _():
            columns = pl.ds(pl.multiple_of(mine * BLOCK, BLOCK), BLOCK)
            own = [own_ref[c : c + 1, columns] for c in range(6)]
            sums = cell(own, cols_ref, (i // CODES) * FB_DEV + other, count.astype(F32), as_target)
            for f, value in enumerate(sums):
                acc_ref[f, :, columns] += value

        return carry

    lax.fori_loop(0, slots, visit, 0)

    scale = scale_ref[0, 0]
    for at, o in enumerate(own_blocks):
        columns = slice(o * BLOCK, (o + 1) * BLOCK)
        sums = [jnp.sum(acc_ref[f, :, columns], axis=0, keepdims=True) for f in range(8 if as_target else 7)]
        weight = scale * own_ref[6:7, columns]
        target = slice(at * BLOCK, (at + 1) * BLOCK)
        for c in range(3):
            lever = own_ref[3 + c : 4 + c, columns] * sums[4] if as_target else sums[4 + c]
            center = weight * (2.0 * lever - 4.0 * sums[1 + c])
            normal = 2.0 * weight * sums[5 + c] if as_target else jnp.zeros_like(weight)
            if as_target:
                center = center + base_ref[c : c + 1, columns]
            out_ref[c : c + 1, target] = center
            out_ref[3 + c : 4 + c, target] = normal
        area = scale * sums[0]
        if as_target:
            area = area + base_ref[6:7, columns]
        out_ref[6:7, target] = area
        out_ref[7:8, target] = jnp.zeros_like(area)


def pair_sums(as_target, own_blocks, codes, scale, own, partners, base, name):
    group = len(partners)
    cells = group * CODES * len(own_blocks) // FB_DEV // 3
    return pl.pallas_call(
        functools.partial(pair_kernel, as_target, own_blocks, group),
        out_shape=jax.ShapeDtypeStruct((8, len(own_blocks) * BLOCK), F32),
        in_specs=[SMEM, SMEM] + [VMEM] * (group + 2),
        out_specs=VMEM,
        scratch_shapes=[
            pltpu.VMEM((group * FB_DEV, BLOCK, 128), F32),
            pltpu.VMEM((8, 8, FB_DEV * BLOCK), F32),
            pltpu.SMEM((group * CODES,), jnp.int32),
        ],
        compiler_params=pltpu.CompilerParams(vmem_limit_bytes=24 * 1024 * 1024),
        cost_estimate=pl.CostEstimate(
            flops=cells * BLOCK * BLOCK * 40, bytes_accessed=1 << 18, transcendentals=cells * BLOCK * BLOCK
        ),
        name=name,
    )(codes, scale, own, *partners, base)


def incidence_kernel(corner_ref, out_ref):
    verts, faces = out_ref.shape
    vertex = lax.broadcasted_iota(jnp.int32, (verts, 128), 0)
    for e in range(0, faces, 128):
        total = jnp.zeros((verts, 128), F32)
        for k in range(3):
            total = total + jnp.where(corner_ref[k : k + 1, e : e + 128] == vertex, 1.0, 0.0)
        out_ref[:, e : e + 128] = total.astype(jnp.bfloat16)


def incidence_table(corner, verts):
    faces = corner.shape[1]
    return pl.pallas_call(
        incidence_kernel,
        out_shape=jax.ShapeDtypeStruct((verts, faces), jnp.bfloat16),
        in_specs=[VMEM],
        out_specs=VMEM,
        compiler_params=pltpu.CompilerParams(vmem_limit_bytes=16 * 1024 * 1024),
        cost_estimate=pl.CostEstimate(flops=verts * faces * 9, bytes_accessed=verts * faces * 2, transcendentals=0),
        name="incidence",
    )(corner)


def thirds(values):
    high = values.astype(jnp.bfloat16)
    rest = values - high.astype(F32)
    middle = rest.astype(jnp.bfloat16)
    low = (rest - middle.astype(F32)).astype(jnp.bfloat16)
    return [high, middle, low]


def finish_kernel(parts_ref, table_ref, vertex_ref, face_ref):
    total = parts_ref[0]
    for i in range(1, parts_ref.shape[0]):
        total = total + parts_ref[i]
    faces = total.shape[1]
    width = 2 * HALO_FACES
    face_ref[...] = total[3:7]
    edge = jnp.concatenate([total[7:8, c * width : (c + 1) * width] for c in range(3)], axis=0)
    contract = (((1,), (1,)), ((), ()))
    out = jnp.zeros((3, vertex_ref.shape[1]), F32)
    for high, side in zip(thirds(total[0:3]), thirds(edge)):
        out = out + lax.dot_general(high, table_ref[:, 0:faces], contract, preferred_element_type=F32)
        out = out + lax.dot_general(side, table_ref[:, faces:], contract, preferred_element_type=F32)
    vertex_ref[...] = out / 3.0


def finish(parts, table):
    verts, faces = table.shape[0], parts.shape[2]
    return pl.pallas_call(
        finish_kernel,
        out_shape=(jax.ShapeDtypeStruct((3, verts), F32), jax.ShapeDtypeStruct((4, faces), F32)),
        in_specs=[VMEM, VMEM],
        out_specs=(VMEM, VMEM),
        compiler_params=pltpu.CompilerParams(vmem_limit_bytes=16 * 1024 * 1024),
        name="finish",
    )(parts, table)


def shards(centroids, normals, areas, cotangent, pair_code, corner_vertex):
    count, shares = lax.axis_size("blk"), lax.axis_size("pair")
    group = count // shares
    both = ("blk", "pair")
    blk = lax.axis_index("blk")
    faces = centroids.shape[1]

    def route(k):
        pairs = []
        for b in range(count):
            for p in range(shares):
                q = group * p + (b + k) % group
                pairs.append((q * shares + b // group, b * shares + p))
        return pairs

    own = jnp.concatenate([centroids, normals, areas[None], jnp.zeros((1, faces), F32)], axis=0)
    partners = [lax.ppermute(own, both, route(k)) for k in range(group)]
    held = lax.all_to_all(pair_code.reshape(shares, group), "pair", 0, 0, tiled=True).T
    held_twice = jnp.concatenate([held, held], axis=0)
    lane = blk % group
    codes_out = lax.dynamic_slice_in_dim(held_twice, lane, group, axis=0)
    codes_in = jnp.concatenate(
        [
            lax.ppermute(lax.dynamic_slice_in_dim(held, (blk + group - k) % group, 1, axis=0), both, route(k))
            for k in range(group)
        ],
        axis=0,
    )
    scale = cotangent.reshape(1, 1)
    corner = jnp.concatenate(
        [corner_vertex[:, HALO_FACES:-HALO_FACES], corner_vertex[:, :HALO_FACES], corner_vertex[:, -HALO_FACES:]], axis=1
    )
    table = incidence_table(corner, faces // 2)

    sent = pair_sums(False, (0, 1, 2, 3), codes_out, scale, own, partners, own, "source_role")
    outer = pair_sums(True, (0, 3), codes_in, scale, own, partners, sent, "target_role_outer")
    head, tail = outer[0:3, :HALO_FACES], outer[0:3, -HALO_FACES:]
    forward = [(i, (i + 1) % count) for i in range(count)]
    left = lax.ppermute(tail, "blk", forward)
    right = lax.ppermute(head, "blk", [(j, i) for i, j in forward])
    inner = pair_sums(True, (1, 2), codes_in, scale, own, partners, sent, "target_role_inner")
    edge = jnp.concatenate([left, right], axis=1).reshape(1, -1)
    edge = jnp.pad(edge, ((0, 0), (0, faces - edge.shape[1])))
    part = jnp.concatenate([outer[:, :BLOCK], inner, outer[:, BLOCK:]], axis=1)
    part = jnp.concatenate([part[:7], edge], axis=0)
    parts = lax.all_gather(part, "pair")
    return finish(parts, table)


def solution(mesh):
    placed = (
        P(None, "blk"),
        P(None, "blk"),
        P("blk"),
        P(),
        P("blk", "pair", None, None),
        P(None, "blk"),
    )
    return jax.shard_map(
        shards,
        mesh=mesh,
        in_specs=placed,
        out_specs=(P(None, "blk"), P(None, "blk")),
        check_vma=False,
    )
```

```python
import functools

import jax
import jax.numpy as jnp
from jax import lax
from jax.experimental import pallas as pl
from jax.experimental.pallas import tpu as pltpu
from jax.sharding import PartitionSpec as P

BLOCK = 256
FB_DEV = 4
HALO_FACES = 64
CODES = FB_DEV * FB_DEV
DEPTH = 64
CELLS = 2
LEFT = (0, 0, 1, 1, 0, 2)
RIGHT = (0, 1, 0, 1, 2, 0)
ONES = (0, 1, 4)
F32 = jnp.float32
BF16 = jnp.bfloat16
VMEM = pl.BlockSpec(memory_space=pltpu.VMEM)
SMEM = pl.BlockSpec(memory_space=pltpu.SMEM)
dot = functools.partial(jnp.dot, preferred_element_type=F32)


def thirds(values):
    high = values.astype(BF16).astype(F32)
    rest = values - high
    middle = rest.astype(BF16).astype(F32)
    return [high, middle, (rest - middle).astype(BF16).astype(F32)]


def square(x):
    return jnp.sum(x[0:3] * x[0:3], axis=0, keepdims=True)


def lever(x):
    return jnp.sum(x[0:3] * x[3:6], axis=0, keepdims=True)


def partner_features(partners, left_ref, feat_ref):
    width = FB_DEV * BLOCK
    row = lax.broadcasted_iota(jnp.int32, (8, width), 0)
    for k, partner in enumerate(partners):
        x = partner[...]
        area = x[6:7]
        x = jnp.where(row >= 6, 1.0, x)
        split = thirds(x)
        extra = thirds(square(x)) + thirds(lever(x)) + [jnp.zeros((10, width), F32)]
        left = jnp.concatenate([split[i] for i in LEFT] + extra, axis=0)
        feat = jnp.concatenate(thirds(x * area) + [jnp.zeros((8, width), F32)], axis=0).astype(BF16)
        for s in range(FB_DEV):
            columns = slice(s * BLOCK, (s + 1) * BLOCK)
            left_ref[k * FB_DEV + s] = left[:, columns].T.astype(BF16)
            feat_ref[k * FB_DEV + s] = feat[:, columns]


def own_features(own_ref, own_blocks, right_ref):
    row = lax.broadcasted_iota(jnp.int32, (8, BLOCK), 0)
    zero = jnp.zeros((8, BLOCK), F32)
    first, second = row < 3, jnp.logical_and(row >= 3, row < 6)
    for a, o in enumerate(own_blocks):
        x = own_ref[:, o * BLOCK : (o + 1) * BLOCK]
        center = thirds(-2.0 * x)
        swapped = thirds(jnp.concatenate([x[3:6], x[0:3], x[6:8]], axis=0))
        distance, level = thirds(square(x) + 1.0), thirds(lever(x))
        sides = (
            [jnp.where(first, center[i], zero) for i in RIGHT],
            [jnp.where(first, -swapped[i], zero) for i in RIGHT],
            [jnp.where(second, swapped[i], zero) for i in RIGHT],
        )
        for i, g in enumerate(ONES):
            sides[0][g] = jnp.where(row == 7, distance[i], sides[0][g])
            sides[1][g] = jnp.where(row == 7, level[i], sides[1][g])
        tails = (jnp.where(first, 1.0, zero), zero, jnp.where(second, -1.0, zero))
        for m in range(3):
            right_ref[a, m] = jnp.concatenate(sides[m] + [tails[m], zero], axis=0).astype(BF16)


def list_cells(own_blocks, group, place_ref, count_ref, list_ref):
    slots = group * CODES
    lane = place_ref[0, 0]

    def step(i, found):
        role, j = i // slots, i % slots
        k, code = j // CODES, j % CODES
        line = jnp.where(role == 0, k, group)
        member = jnp.where(role == 0, lane, (lane + k) % group)
        count = count_ref[line, member * CODES + code].astype(jnp.int32)
        first, second = code // FB_DEV, code % FB_DEV
        mine, other = jnp.where(role == 0, first, second), jnp.where(role == 0, second, first)
        at, held = jnp.int32(0), jnp.bool_(False)
        for a, o in enumerate(own_blocks):
            at, held = jnp.where(mine == o, a, at), jnp.logical_or(held, mine == o)
        list_ref[found] = count * 65536 + role * 4096 + at * 256 + k * FB_DEV + other
        return found + jnp.logical_and(count > 0, held).astype(jnp.int32)

    found = lax.fori_loop(0, 2 * slots, step, jnp.int32(0), unroll=4)
    for u in range(CELLS):
        list_ref[found + u] = 0
    return found


def weighted(feat, values):
    high = values.astype(BF16)
    return dot(feat, high) + dot(feat, (values - high.astype(F32)).astype(BF16))


def cell(entry, left_ref, feat_ref, right_ref):
    count, role, at, x = entry // 65536, (entry // 4096) % 16, (entry // 256) % 16, entry % 256
    left, feat = left_ref[x], feat_ref[x]
    inverse = pl.reciprocal(dot(left, right_ref[at, 0]), approx=True)
    projected = dot(left, right_ref[at, 1 + role])
    scaled = inverse * inverse
    kernel = (projected * projected + 1.0) * scaled
    sums = [weighted(feat, v) for v in (kernel, kernel * inverse, projected * scaled)]
    return at, role, [count.astype(F32) * s for s in sums]


def pair_body(own_blocks, group, place_ref, count_ref, scale_ref, own_ref, left_ref, feat_ref, out_ref, right_ref, acc_ref, list_ref):
    found = list_cells(own_blocks, group, place_ref, count_ref, list_ref)
    own_features(own_ref, own_blocks, right_ref)
    acc_ref[...] = jnp.zeros_like(acc_ref)

    def visit(i, carry):
        results = [cell(list_ref[i * CELLS + u], left_ref, feat_ref, right_ref) for u in range(CELLS)]
        for at, role, sums in results:
            acc_ref[at, 0] += sums[0]
            acc_ref[at, 1] += sums[1]
            acc_ref[at, 2 + role] += sums[2]
        return carry

    lax.fori_loop(0, (found + CELLS - 1) // CELLS, visit, 0)

    scale = scale_ref[0, 0]
    for a, o in enumerate(own_blocks):
        kernel, pushing, target, source = (acc_ref[a, m, 0:8] + acc_ref[a, m, 8:16] + acc_ref[a, m, 16:24] for m in range(4))
        x = own_ref[:, o * BLOCK : (o + 1) * BLOCK]
        center, normal = x[0:3], x[3:6]
        weight = scale * x[6:7]
        push = center * pushing[6:7] - pushing[0:3]
        pull = normal * target[6:7] + source[3:6]
        columns = slice(a * BLOCK, (a + 1) * BLOCK)
        out_ref[0:3, columns] = weight * (2.0 * pull - 4.0 * push)
        out_ref[3:6, columns] = 2.0 * weight * (center * target[6:7] - target[0:3])
        out_ref[6:7, columns] = scale * kernel[6:7]
        out_ref[7:8, columns] = jnp.zeros((1, BLOCK), F32)


def outer_kernel(own_blocks, group, place_ref, count_ref, scale_ref, own_ref, *refs):
    partners, (out_ref, left_ref, feat_ref, *scratch) = refs[:group], refs[group:]
    partner_features(partners, left_ref, feat_ref)
    pair_body(own_blocks, group, place_ref, count_ref, scale_ref, own_ref, left_ref, feat_ref, out_ref, *scratch)


def pair_call(body, own_blocks, group, outputs, operands, name):
    n = len(own_blocks)
    cells = 2 * group * CODES * n // FB_DEV // 3
    in_specs = [SMEM] * 3 + [VMEM] * (len(operands) - 3)
    return pl.pallas_call(
        functools.partial(body, own_blocks, group),
        out_shape=outputs,
        in_specs=in_specs,
        out_specs=jax.tree.map(lambda _: VMEM, outputs),
        scratch_shapes=[
            pltpu.VMEM((n, 3, DEPTH, BLOCK), BF16),
            pltpu.VMEM((n, 4, 32, BLOCK), F32),
            pltpu.SMEM((2 * group * CODES + 8,), jnp.int32),
        ],
        compiler_params=pltpu.CompilerParams(vmem_limit_bytes=24 * 1024 * 1024),
        cost_estimate=pl.CostEstimate(
            flops=cells * BLOCK * BLOCK * 500, bytes_accessed=1 << 21, transcendentals=cells * BLOCK * BLOCK
        ),
        name=name,
    )(*operands)


def incidence_kernel(corner_ref, out_ref):
    verts, faces = out_ref.shape
    vertex = lax.broadcasted_iota(jnp.int32, (verts, 128), 0)
    for e in range(0, faces, 128):
        total = jnp.zeros((verts, 128), F32)
        for k in range(3):
            total = total + jnp.where(corner_ref[k : k + 1, e : e + 128] == vertex, 1.0, 0.0)
        out_ref[:, e : e + 128] = total.astype(BF16)


def incidence_table(corner, verts):
    faces = corner.shape[1]
    return pl.pallas_call(
        incidence_kernel,
        out_shape=jax.ShapeDtypeStruct((verts, faces), BF16),
        in_specs=[VMEM],
        out_specs=VMEM,
        compiler_params=pltpu.CompilerParams(vmem_limit_bytes=16 * 1024 * 1024),
        cost_estimate=pl.CostEstimate(flops=verts * faces * 9, bytes_accessed=verts * faces * 2, transcendentals=0),
        name="incidence",
    )(corner)


def finish_kernel(parts_ref, table_ref, vertex_ref, face_ref):
    total = parts_ref[0]
    for i in range(1, parts_ref.shape[0]):
        total = total + parts_ref[i]
    faces = total.shape[1]
    width = 2 * HALO_FACES
    face_ref[...] = total[3:7]
    edge = jnp.concatenate([total[7:8, c * width : (c + 1) * width] for c in range(3)], axis=0)
    contract = (((1,), (1,)), ((), ()))
    out = jnp.zeros((3, vertex_ref.shape[1]), F32)
    for main, side in zip(thirds(total[0:3]), thirds(edge)):
        out = out + lax.dot_general(main.astype(BF16), table_ref[:, 0:faces], contract, preferred_element_type=F32)
        out = out + lax.dot_general(side.astype(BF16), table_ref[:, faces:], contract, preferred_element_type=F32)
    vertex_ref[...] = out / 3.0


def finish(parts, table):
    verts, faces = table.shape[0], parts.shape[2]
    return pl.pallas_call(
        finish_kernel,
        out_shape=(jax.ShapeDtypeStruct((3, verts), F32), jax.ShapeDtypeStruct((4, faces), F32)),
        in_specs=[VMEM, VMEM],
        out_specs=(VMEM, VMEM),
        compiler_params=pltpu.CompilerParams(vmem_limit_bytes=16 * 1024 * 1024),
        name="finish",
    )(parts, table)


def shards(centroids, normals, areas, cotangent, pair_code, corner_vertex):
    count, shares = lax.axis_size("blk"), lax.axis_size("pair")
    group = count // shares
    both = ("blk", "pair")
    faces = centroids.shape[1]

    def route(k):
        pairs = []
        for b in range(count):
            for p in range(shares):
                q = group * p + (b + k) % group
                pairs.append((q * shares + b // group, b * shares + p))
        return pairs

    held = lax.all_to_all(pair_code.reshape(shares, group), "pair", 0, 0, tiled=True)
    tally = jnp.sum((held[:, :, None] == jnp.arange(CODES, dtype=jnp.int32)).astype(F32), axis=0).reshape(1, group * CODES)
    tally_row = jnp.pad(tally, ((0, 0), (0, faces - group * CODES)))
    own = jnp.concatenate([centroids, normals, areas[None], tally_row], axis=0)
    partners = [lax.ppermute(own, both, route(k)) for k in range(group)]
    counts = jnp.concatenate([x[7:8, : group * CODES] for x in partners] + [tally], axis=0)
    place = (lax.axis_index("blk") % group).reshape(1, 1)
    scale = cotangent.reshape(1, 1)
    corner = jnp.concatenate(
        [corner_vertex[:, HALO_FACES:-HALO_FACES], corner_vertex[:, :HALO_FACES], corner_vertex[:, -HALO_FACES:]], axis=1
    )
    table = incidence_table(corner, faces // 2)

    half = jax.ShapeDtypeStruct((8, faces // 2), F32)
    left = jax.ShapeDtypeStruct((group * FB_DEV, BLOCK, DEPTH), BF16)
    feat = jax.ShapeDtypeStruct((group * FB_DEV, 32, BLOCK), BF16)
    outer, left, feat = pair_call(
        outer_kernel, (0, 3), group, (half, left, feat), (place, counts, scale, own, *partners), "outer_blocks"
    )
    head, tail = outer[0:3, :HALO_FACES], outer[0:3, -HALO_FACES:]
    forward = [(i, (i + 1) % count) for i in range(count)]
    before = lax.ppermute(tail, "blk", forward)
    after = lax.ppermute(head, "blk", [(j, i) for i, j in forward])
    inner = pair_call(pair_body, (1, 2), group, half, (place, counts, scale, own, left, feat), "inner_blocks")
    edge = jnp.concatenate([before, after], axis=1).reshape(1, -1)
    edge = jnp.pad(edge, ((0, 0), (0, faces - edge.shape[1])))
    part = jnp.concatenate([outer[:, :BLOCK], inner, outer[:, BLOCK:]], axis=1)
    part = jnp.concatenate([part[:7], edge], axis=0)
    parts = lax.all_gather(part, "pair")
    return finish(parts, table)


def solution(mesh):
    placed = (
        P(None, "blk"),
        P(None, "blk"),
        P("blk"),
        P(),
        P("blk", "pair", None, None),
        P(None, "blk"),
    )
    return jax.shard_map(
        shards,
        mesh=mesh,
        in_specs=placed,
        out_specs=(P(None, "blk"), P(None, "blk")),
        check_vma=False,
    )
```

```python
import functools

import jax
import jax.numpy as jnp
from jax import lax
from jax.experimental import pallas as pl
from jax.experimental.pallas import tpu as pltpu
from jax.sharding import PartitionSpec as P

BLOCK = 256
FB_DEV = 4
HALO_FACES = 64
CODES = FB_DEV * FB_DEV
DEPTH = 64
LEFT = (0, 0, 1, 1, 0, 2)
RIGHT = (0, 1, 0, 1, 2, 0)
ONES = (0, 1, 4)
F32 = jnp.float32
BF16 = jnp.bfloat16
VMEM = pl.BlockSpec(memory_space=pltpu.VMEM)
SMEM = pl.BlockSpec(memory_space=pltpu.SMEM)
dot = functools.partial(jnp.dot, preferred_element_type=F32)


def thirds(values):
    high = values.astype(BF16).astype(F32)
    rest = values - high
    middle = rest.astype(BF16).astype(F32)
    return [high, middle, (rest - middle).astype(BF16).astype(F32)]


def square(x):
    return jnp.sum(x[0:3] * x[0:3], axis=0, keepdims=True)


def lever(x):
    return jnp.sum(x[0:3] * x[3:6], axis=0, keepdims=True)


def partner_features(group, first, rows_ref, left_ref, feat_ref):
    width = FB_DEV * BLOCK
    row = lax.broadcasted_iota(jnp.int32, (8, width), 0)
    for k in range(group):
        x = rows_ref[first + k]
        area = x[6:7]
        x = jnp.where(row >= 6, 1.0, x)
        split = thirds(x)
        extra = thirds(square(x)) + thirds(lever(x)) + [jnp.zeros((10, width), F32)]
        left = jnp.concatenate([split[i] for i in LEFT] + extra, axis=0)
        feat = jnp.concatenate(thirds(x * area) + [jnp.zeros((8, width), F32)], axis=0).astype(BF16)
        for s in range(FB_DEV):
            columns = slice(s * BLOCK, (s + 1) * BLOCK)
            left_ref[k * FB_DEV + s] = left[:, columns].T.astype(BF16)
            feat_ref[k * FB_DEV + s] = feat[:, columns]


def own_features(own_ref, own_blocks, right_ref):
    row = lax.broadcasted_iota(jnp.int32, (8, BLOCK), 0)
    zero = jnp.zeros((8, BLOCK), F32)
    first, second = row < 3, jnp.logical_and(row >= 3, row < 6)
    for a, o in enumerate(own_blocks):
        x = own_ref[:, o * BLOCK : (o + 1) * BLOCK]
        center = thirds(-2.0 * x)
        swapped = thirds(jnp.concatenate([x[3:6], x[0:3], x[6:8]], axis=0))
        distance, level = thirds(square(x) + 1.0), thirds(lever(x))
        sides = (
            [jnp.where(first, center[i], zero) for i in RIGHT],
            [jnp.where(first, -swapped[i], zero) for i in RIGHT],
            [jnp.where(second, swapped[i], zero) for i in RIGHT],
        )
        for i, g in enumerate(ONES):
            sides[0][g] = jnp.where(row == 7, distance[i], sides[0][g])
            sides[1][g] = jnp.where(row == 7, level[i], sides[1][g])
        tails = (jnp.where(first, 1.0, zero), zero, jnp.where(second, -1.0, zero))
        for m in range(3):
            right_ref[a, m] = jnp.concatenate(sides[m] + [tails[m], zero], axis=0).astype(BF16)


def list_cells(own_blocks, group, place_ref, count_ref, list_ref):
    n = len(own_blocks)
    lane, core = place_ref[0, 0], place_ref[0, 1]
    last = count_ref.shape[0] - 1
    list_ref[0] = 0

    def step(j, found):
        k, a, other = j // (n * FB_DEV), (j // FB_DEV) % n, j % FB_DEV
        mine = sum(jnp.where(a == i, o, 0) for i, o in enumerate(own_blocks))
        partner = core * group + k
        place = a * 256 + k * FB_DEV + other
        target = count_ref[partner, lane * CODES + mine * FB_DEV + other].astype(jnp.int32)
        list_ref[found + 1] = target * 65536 + place
        found = found + (target > 0).astype(jnp.int32)
        source = count_ref[last, partner * CODES + other * FB_DEV + mine].astype(jnp.int32)
        list_ref[found + 1] = source * 65536 + 4096 + place
        return found + (source > 0).astype(jnp.int32)

    found = lax.fori_loop(0, group * n * FB_DEV, step, jnp.int32(0), unroll=4)
    for u in range(3):
        list_ref[found + 1 + u] = 0
    return found


def unpack(entry):
    return entry // 65536, (entry // 4096) % 16, (entry // 256) % 16, entry % 256


def products(entry, left_ref, right_ref, out_ref):
    _, role, at, x = unpack(entry)
    left = left_ref[x]
    out_ref[0] = dot(left, right_ref[at, 0])
    out_ref[1] = dot(left, right_ref[at, 1 + role])


def weights(in_ref, out_ref):
    inverse = pl.reciprocal(in_ref[0], approx=True)
    projected = in_ref[1]
    scaled = inverse * inverse
    kernel = (projected * projected + 1.0) * scaled
    for m, values in enumerate((kernel, kernel * inverse, projected * scaled)):
        high = values.astype(BF16)
        out_ref[m, 0] = high
        out_ref[m, 1] = (values - high.astype(F32)).astype(BF16)


def reduce_cell(entry, feat_ref, in_ref, acc_ref):
    count, role, at, x = unpack(entry)
    feat = feat_ref[x]
    for m, place in enumerate((0, 1, 2 + role)):
        acc_ref[at, place] += count.astype(F32) * (dot(feat, in_ref[m, 0]) + dot(feat, in_ref[m, 1]))


def pair_body(own_blocks, group, place_ref, count_ref, scale_ref, own_ref, left_ref, feat_ref, out_ref, right_ref, acc_ref, list_ref, *stages):
    product_refs, weight_refs = stages[:2], stages[2:]
    found = list_cells(own_blocks, group, place_ref, count_ref, list_ref)
    own_features(own_ref, own_blocks, right_ref)
    acc_ref[...] = jnp.zeros_like(acc_ref)
    weight_refs[1][...] = jnp.zeros_like(weight_refs[1])
    products(list_ref[1], left_ref, right_ref, product_refs[0])

    def visit(i, carry):
        for u in range(2):
            now, later = u, 1 - u
            reduce_cell(list_ref[2 * i + u], feat_ref, weight_refs[later], acc_ref)
            weights(product_refs[now], weight_refs[now])
            products(list_ref[2 * i + u + 2], left_ref, right_ref, product_refs[later])
        return carry

    rounds = (found + 1) // 2
    lax.fori_loop(0, rounds, visit, 0)
    reduce_cell(list_ref[2 * rounds], feat_ref, weight_refs[1], acc_ref)

    scale = scale_ref[0, 0]
    for a, o in enumerate(own_blocks):
        kernel, pushing, target, source = (acc_ref[a, m, 0:8] + acc_ref[a, m, 8:16] + acc_ref[a, m, 16:24] for m in range(4))
        x = own_ref[:, o * BLOCK : (o + 1) * BLOCK]
        center, normal = x[0:3], x[3:6]
        weight = scale * x[6:7]
        push = center * pushing[6:7] - pushing[0:3]
        pull = normal * target[6:7] + source[3:6]
        columns = slice(a * BLOCK, (a + 1) * BLOCK)
        out_ref[0:3, columns] = weight * (2.0 * pull - 4.0 * push)
        out_ref[3:6, columns] = 2.0 * weight * (center * target[6:7] - target[0:3])
        out_ref[6:7, columns] = scale * kernel[6:7]
        out_ref[7:8, columns] = jnp.zeros((1, BLOCK), F32)


def outer_kernel(own_blocks, group, place_ref, count_ref, scale_ref, own_ref, rows_ref, out_ref, left_ref, feat_ref, *scratch):
    partner_features(group, place_ref[0, 1] * group, rows_ref, left_ref, feat_ref)
    pair_body(own_blocks, group, place_ref, count_ref, scale_ref, own_ref, left_ref, feat_ref, out_ref, *scratch)


def pair_call(body, own_blocks, group, outputs, operands, name):
    n = len(own_blocks)
    cells = 2 * group * CODES * n // FB_DEV // 3
    in_specs = [SMEM] * 3 + [VMEM] * (len(operands) - 3)
    return pl.pallas_call(
        functools.partial(body, own_blocks, group),
        out_shape=outputs,
        in_specs=in_specs,
        out_specs=jax.tree.map(lambda _: VMEM, outputs),
        scratch_shapes=[
            pltpu.VMEM((n, 3, DEPTH, BLOCK), BF16),
            pltpu.VMEM((n, 4, 32, BLOCK), F32),
            pltpu.SMEM((2 * group * CODES + 8,), jnp.int32),
        ]
        + [pltpu.VMEM((2, BLOCK, BLOCK), F32)] * 2
        + [pltpu.VMEM((3, 2, BLOCK, BLOCK), BF16)] * 2,
        compiler_params=pltpu.CompilerParams(vmem_limit_bytes=24 * 1024 * 1024),
        cost_estimate=pl.CostEstimate(
            flops=cells * BLOCK * BLOCK * 500, bytes_accessed=1 << 21, transcendentals=cells * BLOCK * BLOCK
        ),
        name=name,
    )(*operands)


def incidence_kernel(corner_ref, out_ref):
    verts, faces = out_ref.shape
    vertex = lax.broadcasted_iota(jnp.int32, (verts, 128), 0)
    for e in range(0, faces, 128):
        total = jnp.zeros((verts, 128), F32)
        for k in range(3):
            total = total + jnp.where(corner_ref[k : k + 1, e : e + 128] == vertex, 1.0, 0.0)
        out_ref[:, e : e + 128] = total.astype(BF16)


def incidence_table(corner, verts):
    faces = corner.shape[1]
    return pl.pallas_call(
        incidence_kernel,
        out_shape=jax.ShapeDtypeStruct((verts, faces), BF16),
        in_specs=[VMEM],
        out_specs=VMEM,
        compiler_params=pltpu.CompilerParams(vmem_limit_bytes=16 * 1024 * 1024),
        cost_estimate=pl.CostEstimate(flops=verts * faces * 9, bytes_accessed=verts * faces * 2, transcendentals=0),
        name="incidence",
    )(corner)


def finish_kernel(parts_ref, table_ref, vertex_ref, face_ref):
    total = parts_ref[0]
    for i in range(1, parts_ref.shape[0]):
        total = total + parts_ref[i]
    faces = total.shape[1]
    width = 2 * HALO_FACES
    face_ref[...] = total[3:7]
    edge = jnp.concatenate([total[7:8, c * width : (c + 1) * width] for c in range(3)], axis=0)
    contract = (((1,), (1,)), ((), ()))
    out = jnp.zeros((3, vertex_ref.shape[1]), F32)
    for main, side in zip(thirds(total[0:3]), thirds(edge)):
        out = out + lax.dot_general(main.astype(BF16), table_ref[:, 0:faces], contract, preferred_element_type=F32)
        out = out + lax.dot_general(side.astype(BF16), table_ref[:, faces:], contract, preferred_element_type=F32)
    vertex_ref[...] = out / 3.0


def finish(parts, table):
    verts, faces = table.shape[0], parts.shape[2]
    return pl.pallas_call(
        finish_kernel,
        out_shape=(jax.ShapeDtypeStruct((3, verts), F32), jax.ShapeDtypeStruct((4, faces), F32)),
        in_specs=[VMEM, VMEM],
        out_specs=(VMEM, VMEM),
        compiler_params=pltpu.CompilerParams(vmem_limit_bytes=16 * 1024 * 1024),
        name="finish",
    )(parts, table)


def shards(centroids, normals, areas, cotangent, pair_code, corner_vertex):
    count, shares = lax.axis_size("blk"), lax.axis_size("pair")
    side = shares // 2
    group = side // 2
    both = ("blk", "pair")
    faces = centroids.shape[1]
    assert count == side * side
    z, x = lax.axis_index("blk") // side, lax.axis_index("blk") % side
    core = lax.axis_index("pair") % 2

    def at(z, x, y, c):
        return (z * side + x) * shares + y * 2 + c

    every = range(side)
    swap = [(at(y, x, z, c), at(z, x, y, c)) for z in every for x in every for y in every for c in range(2)]
    along = [[z * side + x for x in every] for z in every]

    code = jnp.repeat(pair_code.reshape(side, 1, side), 2, axis=1).reshape(shares, side)
    held = lax.all_to_all(code, "pair", 0, 0, tiled=True)
    tally = jnp.sum((held[:, :, None] == jnp.arange(CODES, dtype=jnp.int32)).astype(F32), axis=0).reshape(1, side * CODES)
    tally_row = jnp.pad(tally, ((0, 0), (0, faces - side * CODES)))
    own = jnp.concatenate([centroids, normals, areas[None], tally_row], axis=0)
    swapped = lax.ppermute(own, both, swap)
    copies = jnp.broadcast_to(swapped[None], (side, 8, faces))
    rows = lax.all_to_all(copies, "blk", 0, 0, axis_index_groups=along)
    counts = jnp.concatenate([rows[:, 7, : side * CODES], tally], axis=0)
    place = jnp.stack([x, core]).reshape(1, 2)
    scale = cotangent.reshape(1, 1)
    corner = jnp.concatenate(
        [corner_vertex[:, HALO_FACES:-HALO_FACES], corner_vertex[:, :HALO_FACES], corner_vertex[:, -HALO_FACES:]], axis=1
    )
    table = incidence_table(corner, faces // 2)

    half = jax.ShapeDtypeStruct((8, faces // 2), F32)
    left = jax.ShapeDtypeStruct((group * FB_DEV, BLOCK, DEPTH), BF16)
    feat = jax.ShapeDtypeStruct((group * FB_DEV, 32, BLOCK), BF16)
    outer, left, feat = pair_call(
        outer_kernel, (0, 3), group, (half, left, feat), (place, counts, scale, own, rows), "outer_blocks"
    )
    head, tail = outer[0:3, :HALO_FACES], outer[0:3, -HALO_FACES:]
    forward = [(i, (i + 1) % count) for i in range(count)]
    before = lax.ppermute(tail, "blk", forward)
    after = lax.ppermute(head, "blk", [(j, i) for i, j in forward])
    inner = pair_call(pair_body, (1, 2), group, half, (place, counts, scale, own, left, feat), "inner_blocks")
    edge = jnp.concatenate([before, after], axis=1).reshape(1, -1)
    edge = jnp.pad(edge, ((0, 0), (0, faces - edge.shape[1])))
    part = jnp.concatenate([outer[:, :BLOCK], inner, outer[:, BLOCK:]], axis=1)
    part = jnp.concatenate([part[:7], edge], axis=0)
    parts = lax.all_gather(part, "pair")
    return finish(parts, table)


def solution(mesh):
    placed = (
        P(None, "blk"),
        P(None, "blk"),
        P("blk"),
        P(),
        P("blk", "pair", None, None),
        P(None, "blk"),
    )
    return jax.shard_map(
        shards,
        mesh=mesh,
        in_specs=placed,
        out_specs=(P(None, "blk"), P(None, "blk")),
        check_vma=False,
    )
```

```python
import functools

import jax
import jax.numpy as jnp
from jax import lax
from jax.experimental import pallas as pl
from jax.experimental.pallas import tpu as pltpu
from jax.sharding import PartitionSpec as P

BLOCK = 256
FB_DEV = 4
HALO_FACES = 64
CODES = FB_DEV * FB_DEV
DEPTH = 64
LEFT = (0, 0, 1, 1, 0, 2)
RIGHT = (0, 1, 0, 1, 2, 0)
ONES = (0, 1, 4)
F32 = jnp.float32
BF16 = jnp.bfloat16
VMEM = pl.BlockSpec(memory_space=pltpu.VMEM)
SMEM = pl.BlockSpec(memory_space=pltpu.SMEM)
dot = functools.partial(jnp.dot, preferred_element_type=F32)


def thirds(values):
    high = values.astype(BF16).astype(F32)
    rest = values - high
    middle = rest.astype(BF16).astype(F32)
    return [high, middle, (rest - middle).astype(BF16).astype(F32)]


def square(x):
    return jnp.sum(x[0:3] * x[0:3], axis=0, keepdims=True)


def lever(x):
    return jnp.sum(x[0:3] * x[3:6], axis=0, keepdims=True)


def partner_features(rows_ref, left_ref, feat_ref):
    width = FB_DEV * BLOCK
    row = lax.broadcasted_iota(jnp.int32, (8, width), 0)
    for k in range(rows_ref.shape[0]):
        x = rows_ref[k]
        area = x[6:7]
        x = jnp.where(row >= 6, 1.0, x)
        split = thirds(x)
        extra = thirds(square(x)) + thirds(lever(x)) + [jnp.zeros((10, width), F32)]
        left = jnp.concatenate([split[i] for i in LEFT] + extra, axis=0).astype(BF16)
        feat = jnp.concatenate(thirds(x * area) + [jnp.zeros((8, width), F32)], axis=0).astype(BF16)
        for s in range(FB_DEV):
            columns = slice(s * BLOCK, (s + 1) * BLOCK)
            left_ref[k * FB_DEV + s] = left[:, columns]
            feat_ref[k * FB_DEV + s] = feat[:, columns]


def own_features(x, right_ref):
    row = lax.broadcasted_iota(jnp.int32, (8, BLOCK), 0)
    zero = jnp.zeros((8, BLOCK), F32)
    first, second = row < 3, jnp.logical_and(row >= 3, row < 6)
    center = thirds(-2.0 * x)
    swapped = thirds(jnp.concatenate([x[3:6], x[0:3], x[6:8]], axis=0))
    distance, level = thirds(square(x) + 1.0), thirds(lever(x))
    sides = (
        [jnp.where(first, center[i], zero) for i in RIGHT],
        [jnp.where(first, -swapped[i], zero) for i in RIGHT],
        [jnp.where(second, swapped[i], zero) for i in RIGHT],
    )
    for i, g in enumerate(ONES):
        sides[0][g] = jnp.where(row == 7, distance[i], sides[0][g])
        sides[1][g] = jnp.where(row == 7, level[i], sides[1][g])
    tails = (jnp.where(first, 1.0, zero), zero, jnp.where(second, -1.0, zero))
    for m in range(3):
        right_ref[m] = jnp.concatenate(sides[m] + [tails[m], zero], axis=0).astype(BF16)


def list_cells(mine, lane, count_ref, list_ref):
    last = count_ref.shape[0] - 1
    list_ref[0] = 0

    def step(j, found):
        partner, other = j // FB_DEV, j % FB_DEV
        target = count_ref[partner, lane * CODES + mine * FB_DEV + other]
        list_ref[found + 1] = target * 65536 + j
        found = found + (target > 0).astype(jnp.int32)
        source = count_ref[last, partner * CODES + other * FB_DEV + mine]
        list_ref[found + 1] = source * 65536 + 256 + j
        return found + (source > 0).astype(jnp.int32)

    found = lax.fori_loop(0, last * FB_DEV, step, jnp.int32(0), unroll=8)
    for u in range(3):
        list_ref[found + 1 + u] = 0
    return found


def unpack(entry):
    return entry // 65536, (entry // 256) % 256, entry % 256


def products(entry, left_ref, right_ref, out_ref):
    _, role, x = unpack(entry)
    left = left_ref[x]
    over = (((0,), (0,)), ((), ()))
    out_ref[0] = lax.dot_general(left, right_ref[0], over, preferred_element_type=F32)
    out_ref[1] = lax.dot_general(left, right_ref[1 + role], over, preferred_element_type=F32)


def weights(entry, rows_ref, in_ref, out_ref, kernel_ref):
    count, _, x = unpack(entry)
    rows = rows_ref[x // FB_DEV, :, pl.ds(pl.multiple_of((x % FB_DEV) * BLOCK, BLOCK), BLOCK)]
    area = rows.T[:, 6:7]
    inverse = pl.reciprocal(in_ref[0], approx=True)
    projected = in_ref[1]
    scaled = inverse * inverse
    kernel = (projected * projected + 1.0) * scaled
    kernel_ref[...] += count.astype(F32) * jnp.sum((kernel * area).reshape(BLOCK // 8, 8, BLOCK), axis=0)
    for m, values in enumerate((kernel * inverse, projected * scaled)):
        high = values.astype(BF16)
        out_ref[m, 0] = high
        out_ref[m, 1] = (values - high.astype(F32)).astype(BF16)


def reduce_cell(entry, feat_ref, in_ref, acc_ref):
    count, role, x = unpack(entry)
    feat = feat_ref[x]
    for m, place in enumerate((0, 1 + role)):
        acc_ref[place] += count.astype(F32) * (dot(feat, in_ref[m, 0]) + dot(feat, in_ref[m, 1]))


def pair_body(mine, place_ref, count_ref, scale_ref, own_ref, rows_ref, left_ref, feat_ref, out_ref, right_ref, acc_ref, kernel_ref, list_ref, *stages):
    product_refs, weight_refs = stages[:2], stages[2:]
    found = list_cells(mine, place_ref[0, 0], count_ref, list_ref)
    own = own_ref[:, pl.ds(pl.multiple_of(mine * BLOCK, BLOCK), BLOCK)]
    own_features(own, right_ref)
    acc_ref[...] = jnp.zeros_like(acc_ref)
    kernel_ref[...] = jnp.zeros_like(kernel_ref)
    weight_refs[1][...] = jnp.zeros_like(weight_refs[1])
    products(list_ref[1], left_ref, right_ref, product_refs[0])

    def visit(i, carry):
        for u in range(2):
            now, later = u, 1 - u
            reduce_cell(list_ref[2 * i + u], feat_ref, weight_refs[later], acc_ref)
            weights(list_ref[2 * i + u + 1], rows_ref, product_refs[now], weight_refs[now], kernel_ref)
            products(list_ref[2 * i + u + 2], left_ref, right_ref, product_refs[later])
        return carry

    rounds = (found + 1) // 2
    lax.fori_loop(0, rounds, visit, 0)
    reduce_cell(list_ref[2 * rounds], feat_ref, weight_refs[1], acc_ref)

    scale = scale_ref[0, 0]
    pushing, target, source = (acc_ref[m, 0:8] + acc_ref[m, 8:16] + acc_ref[m, 16:24] for m in range(3))
    center, normal = own[0:3], own[3:6]
    weight = scale * own[6:7]
    push = center * pushing[6:7] - pushing[0:3]
    pull = normal * target[6:7] + source[3:6]
    out_ref[0:3, :] = weight * (2.0 * pull - 4.0 * push)
    out_ref[3:6, :] = 2.0 * weight * (center * target[6:7] - target[0:3])
    out_ref[6:7, :] = scale * jnp.sum(kernel_ref[...], axis=0, keepdims=True)
    out_ref[7:8, :] = jnp.zeros((1, BLOCK), F32)


def outer_kernel(place_ref, count_ref, scale_ref, own_ref, rows_ref, out_ref, edge_ref, left_ref, feat_ref, *scratch):
    core = place_ref[0, 1]
    partner_features(rows_ref, left_ref, feat_ref)
    pair_body((1 - core) * (FB_DEV - 1), place_ref, count_ref, scale_ref, own_ref, rows_ref, left_ref, feat_ref, out_ref, *scratch)
    gap = jnp.zeros((1, HALO_FACES), F32)
    tails, heads = [], []
    for c in range(3):
        tails += [out_ref[c : c + 1, BLOCK - HALO_FACES :], gap]
        heads += [gap, out_ref[c : c + 1, :HALO_FACES]]
    rest = [gap] * (2 * BLOCK // HALO_FACES - 6)
    edge_ref[...] = jnp.where(core == 0, jnp.concatenate(tails + rest, axis=1), jnp.concatenate(heads + rest, axis=1))


def inner_kernel(place_ref, *refs):
    pair_body(FB_DEV - 2 - place_ref[0, 1], place_ref, *refs)


def pair_call(body, outputs, operands, name):
    partners = operands[1].shape[0] - 1
    cells = 2 * partners * FB_DEV // 3
    in_specs = [SMEM] * 3 + [VMEM] * (len(operands) - 3)
    return pl.pallas_call(
        body,
        out_shape=outputs,
        in_specs=in_specs,
        out_specs=jax.tree.map(lambda _: VMEM, outputs),
        scratch_shapes=[
            pltpu.VMEM((3, DEPTH, BLOCK), BF16),
            pltpu.VMEM((3, 32, BLOCK), F32),
            pltpu.VMEM((8, BLOCK), F32),
            pltpu.SMEM((2 * partners * FB_DEV + 8,), jnp.int32),
        ]
        + [pltpu.VMEM((2, BLOCK, BLOCK), F32)] * 2
        + [pltpu.VMEM((2, 2, BLOCK, BLOCK), BF16)] * 2,
        compiler_params=pltpu.CompilerParams(vmem_limit_bytes=24 * 1024 * 1024),
        cost_estimate=pl.CostEstimate(
            flops=cells * BLOCK * BLOCK * 500, bytes_accessed=1 << 21, transcendentals=cells * BLOCK * BLOCK
        ),
        name=name,
    )(*operands)


def incidence_kernel(corner_ref, out_ref):
    verts, faces = out_ref.shape
    vertex = lax.broadcasted_iota(jnp.int32, (verts, 128), 0)
    for e in range(0, faces, 128):
        total = jnp.zeros((verts, 128), F32)
        for k in range(3):
            total = total + jnp.where(corner_ref[k : k + 1, e : e + 128] == vertex, 1.0, 0.0)
        out_ref[:, e : e + 128] = total.astype(BF16)


def incidence_table(corner, verts):
    faces = corner.shape[1]
    return pl.pallas_call(
        incidence_kernel,
        out_shape=jax.ShapeDtypeStruct((verts, faces), BF16),
        in_specs=[VMEM],
        out_specs=VMEM,
        compiler_params=pltpu.CompilerParams(vmem_limit_bytes=16 * 1024 * 1024),
        cost_estimate=pl.CostEstimate(flops=verts * faces * 9, bytes_accessed=verts * faces * 2, transcendentals=0),
        name="incidence",
    )(corner)


def finish_kernel(parts_ref, table_ref, vertex_ref, face_ref):
    sums = []
    for core in range(2):
        total = parts_ref[core]
        for i in range(core + 2, parts_ref.shape[0], 2):
            total = total + parts_ref[i]
        sums.append(total)
    low, high = sums[1], sums[0]
    total = jnp.concatenate([low[:, :BLOCK], low[:, BLOCK:], high[:, BLOCK:], high[:, :BLOCK]], axis=1)
    faces = total.shape[1]
    width = 2 * HALO_FACES
    face_ref[...] = total[3:7]
    edges = low[7:8] + high[7:8]
    edge = jnp.concatenate([edges[:, c * width : (c + 1) * width] for c in range(3)], axis=0)
    contract = (((1,), (1,)), ((), ()))
    out = jnp.zeros((3, vertex_ref.shape[1]), F32)
    for main, side in zip(thirds(total[0:3]), thirds(edge)):
        out = out + lax.dot_general(main.astype(BF16), table_ref[:, 0:faces], contract, preferred_element_type=F32)
        out = out + lax.dot_general(side.astype(BF16), table_ref[:, faces:], contract, preferred_element_type=F32)
    vertex_ref[...] = out / 3.0


def finish(parts, table):
    verts, faces = table.shape[0], 2 * parts.shape[2]
    return pl.pallas_call(
        finish_kernel,
        out_shape=(jax.ShapeDtypeStruct((3, verts), F32), jax.ShapeDtypeStruct((4, faces), F32)),
        in_specs=[VMEM, VMEM],
        out_specs=(VMEM, VMEM),
        compiler_params=pltpu.CompilerParams(vmem_limit_bytes=16 * 1024 * 1024),
        name="finish",
    )(parts, table)


def shards(centroids, normals, areas, cotangent, pair_code, corner_vertex):
    count, shares = lax.axis_size("blk"), lax.axis_size("pair")
    side = shares // 2
    both = ("blk", "pair")
    faces = centroids.shape[1]
    assert count == side * side
    z, x = lax.axis_index("blk") // side, lax.axis_index("blk") % side
    core = lax.axis_index("pair") % 2

    def at(z, x, y, c):
        return (z * side + x) * shares + y * 2 + c

    every = range(side)
    swap = [(at(y, x, z, c), at(z, x, y, c)) for z in every for x in every for y in every for c in range(2)]
    along = [[z * side + x for x in every] for z in every]

    code = jnp.repeat(pair_code.reshape(side, 1, side), 2, axis=1).reshape(shares, side)
    held = lax.all_to_all(code, "pair", 0, 0, tiled=True)
    tally = jnp.sum((held[:, :, None] == jnp.arange(CODES, dtype=jnp.int32)).astype(F32), axis=0).reshape(1, side * CODES)
    tally_row = jnp.pad(tally, ((0, 0), (0, faces - side * CODES)))
    own = jnp.concatenate([centroids, normals, areas[None], tally_row], axis=0)
    swapped = lax.ppermute(own, both, swap)
    copies = jnp.broadcast_to(swapped[None], (side, 8, faces))
    rows = lax.all_to_all(copies, "blk", 0, 0, axis_index_groups=along)
    counts = jnp.concatenate([rows[:, 7, : side * CODES], tally], axis=0).astype(jnp.int32)
    place = jnp.stack([x, core]).reshape(1, 2)
    scale = cotangent.reshape(1, 1)
    corner = jnp.concatenate(
        [corner_vertex[:, HALO_FACES:-HALO_FACES], corner_vertex[:, :HALO_FACES], corner_vertex[:, -HALO_FACES:]], axis=1
    )
    table = incidence_table(corner, faces // 2)

    block = jax.ShapeDtypeStruct((8, BLOCK), F32)
    row = jax.ShapeDtypeStruct((1, 2 * BLOCK), F32)
    left = jax.ShapeDtypeStruct((side * FB_DEV, DEPTH, BLOCK), BF16)
    feat = jax.ShapeDtypeStruct((side * FB_DEV, 32, BLOCK), BF16)
    outer, edge, left, feat = pair_call(
        outer_kernel, (block, row, left, feat), (place, counts, scale, own, rows), "outer_block"
    )
    hops = [(at(z, x, y, c), (at(z, x, y, c) + (shares if c == 0 else -shares)) % (count * shares))
            for z in every for x in every for y in every for c in range(2)]
    halo = lax.ppermute(edge, both, hops)
    inner = pair_call(inner_kernel, block, (place, counts, scale, own, rows, left, feat), "inner_block")
    part = jnp.concatenate([jnp.concatenate([outer, inner], axis=1)[:7], halo], axis=0)
    parts = lax.all_gather(part, "pair")
    return finish(parts, table)


def solution(mesh):
    placed = (
        P(None, "blk"),
        P(None, "blk"),
        P("blk"),
        P(),
        P("blk", "pair", None, None),
        P(None, "blk"),
    )
    return jax.shard_map(
        shards,
        mesh=mesh,
        in_specs=placed,
        out_specs=(P(None, "blk"), P(None, "blk")),
        check_vma=False,
    )
```

```python
import functools

import jax
import jax.numpy as jnp
from jax import lax
from jax.experimental import pallas as pl
from jax.experimental.pallas import tpu as pltpu
from jax.sharding import PartitionSpec as P

BLOCK = 256
FB_DEV = 4
HALO_FACES = 64
CODES = FB_DEV * FB_DEV
DEPTH = 64
SLICE = 128
LEFT = (0, 0, 1, 1, 0, 2)
RIGHT = (0, 1, 0, 1, 2, 0)
ONES = (0, 1, 4)
F32 = jnp.float32
BF16 = jnp.bfloat16
VMEM = pl.BlockSpec(memory_space=pltpu.VMEM)
SMEM = pl.BlockSpec(memory_space=pltpu.SMEM)
dot = functools.partial(jnp.dot, preferred_element_type=F32)


def thirds(values):
    high = values.astype(BF16).astype(F32)
    rest = values - high
    middle = rest.astype(BF16).astype(F32)
    return [high, middle, (rest - middle).astype(BF16).astype(F32)]


def square(x):
    return jnp.sum(x[0:3] * x[0:3], axis=0, keepdims=True)


def lever(x):
    return jnp.sum(x[0:3] * x[3:6], axis=0, keepdims=True)


def partner_features(rows, left_ref, feat_ref, base):
    x = jnp.concatenate(rows, axis=1)
    width = x.shape[1]
    row = lax.broadcasted_iota(jnp.int32, x.shape, 0)
    area = x[6:7]
    x = jnp.where(row >= 6, 1.0, x)
    split = thirds(x)
    extra = thirds(square(x)) + thirds(lever(x)) + [jnp.zeros((10, width), F32)]
    left = jnp.concatenate([split[i] for i in LEFT] + extra, axis=0).astype(BF16)
    feat = jnp.concatenate(thirds(x * area) + [jnp.zeros((8, width), F32)], axis=0).astype(BF16)
    for i in range(len(rows)):
        columns = slice(i * SLICE, (i + 1) * SLICE)
        left_ref[base + i] = left[:, columns]
        feat_ref[base + i] = feat[:, columns]


def own_features(x, right_ref, at):
    row = lax.broadcasted_iota(jnp.int32, (8, BLOCK), 0)
    zero = jnp.zeros((8, BLOCK), F32)
    first, second = row < 3, jnp.logical_and(row >= 3, row < 6)
    center = thirds(-2.0 * x)
    swapped = thirds(jnp.concatenate([x[3:6], x[0:3], x[6:8]], axis=0))
    distance, level = thirds(square(x) + 1.0), thirds(lever(x))
    sides = (
        [jnp.where(first, center[i], zero) for i in RIGHT],
        [jnp.where(first, -swapped[i], zero) for i in RIGHT],
        [jnp.where(second, swapped[i], zero) for i in RIGHT],
    )
    for i, g in enumerate(ONES):
        sides[0][g] = jnp.where(row == 7, distance[i], sides[0][g])
        sides[1][g] = jnp.where(row == 7, level[i], sides[1][g])
    tails = (jnp.where(first, 1.0, zero), zero, jnp.where(second, -1.0, zero))
    for m in range(3):
        right_ref[at, m] = jnp.concatenate(sides[m] + [tails[m], zero], axis=0).astype(BF16)


def own_block(core, at):
    return jnp.where(core == 0, FB_DEV - 1 - at, at)


def feature_kernel(place_ref, own_ref, rows_ref, left_ref, feat_ref, right_ref):
    for at in range(2):
        first = pl.multiple_of(own_block(place_ref[0, 0], at) * BLOCK, BLOCK)
        own_features(own_ref[:, pl.ds(first, BLOCK)], right_ref, at)
    for k in range(0, rows_ref.shape[0], 8):
        partner_features([rows_ref[k + i] for i in range(8)], left_ref, feat_ref, k)


def features(place, own, rows):
    n = rows.shape[0]
    return pl.pallas_call(
        feature_kernel,
        out_shape=(
            jax.ShapeDtypeStruct((n, DEPTH, SLICE), BF16),
            jax.ShapeDtypeStruct((n, 32, SLICE), BF16),
            jax.ShapeDtypeStruct((2, 3, DEPTH, BLOCK), BF16),
        ),
        in_specs=[SMEM, VMEM, VMEM],
        out_specs=(VMEM, VMEM, VMEM),
        compiler_params=pltpu.CompilerParams(vmem_limit_bytes=16 * 1024 * 1024),
        cost_estimate=pl.CostEstimate(flops=1 << 22, bytes_accessed=1 << 20, transcendentals=0),
        name="features",
    )(place, own, rows)


def tally_kernel(place_ref, held_ref, out_ref):
    other = place_ref[0, 1]
    held = held_ref[...]
    lane = lax.broadcasted_iota(jnp.int32, (1, held.shape[2]), 1)
    for o in range(FB_DEV):
        code = jnp.where(lane < held.shape[2] // 2, o * FB_DEV + other, other * FB_DEV + o)
        out_ref[o : o + 1, :] = jnp.sum(jnp.where(held == code[None], 1.0, 0.0), axis=0).astype(jnp.int32)


def tally(place, held):
    return pl.pallas_call(
        tally_kernel,
        out_shape=jax.ShapeDtypeStruct((FB_DEV, held.shape[2]), jnp.int32),
        in_specs=[SMEM, VMEM],
        out_specs=VMEM,
        compiler_params=pltpu.CompilerParams(vmem_limit_bytes=16 * 1024 * 1024),
        name="tally",
    )(place, held)


def list_cells(mine, count_ref, list_ref):
    list_ref[0] = 0
    list_ref[1] = 0
    found = jnp.int32(0)
    for role in range(2):

        def step(q, found):
            count = count_ref[mine, role * (count_ref.shape[1] // 2) + q]
            list_ref[found + 2] = count * 65536 + role * 256 + q
            return found + (count > 0).astype(jnp.int32)

        found = lax.fori_loop(0, count_ref.shape[1] // 2, step, found, unroll=16)
        list_ref[found + 2] = role * 256
        found = (found + 1) // 2 * 2
    for u in range(6):
        list_ref[found + 2 + u] = 0
    return found // 2


def unpack(entry):
    return entry // 65536, (entry // 256) % 256, entry % 256


def both(ref, list_ref, step):
    return jnp.concatenate([ref[list_ref[2 * step + h] % 256] for h in range(2)], axis=1)


def products(step, list_ref, left_ref, right_ref, at, out_ref):
    role = unpack(list_ref[2 * step])[1]
    left = both(left_ref, list_ref, step)
    over = (((0,), (0,)), ((), ()))
    out_ref[0] = lax.dot_general(left, right_ref[at, 0], over, preferred_element_type=F32)
    out_ref[1] = lax.dot_general(left, right_ref[at, 1 + role], over, preferred_element_type=F32)


def weights(step, list_ref, rows_ref, in_ref, out_ref, kernel_ref):
    for h in range(2):
        count, _, x = unpack(list_ref[2 * step + h])
        area = rows_ref[x].T[:, 6:7]
        here = slice(h * SLICE, (h + 1) * SLICE)
        inverse = pl.reciprocal(in_ref[0, here], approx=True)
        projected = in_ref[1, here]
        scaled = inverse * inverse * count.astype(F32)
        kernel = (projected * projected + 1.0) * scaled
        kernel_ref[...] += jnp.sum((kernel * area).reshape(SLICE // 8, 8, BLOCK), axis=0)
        for m, values in enumerate((kernel * inverse, projected * scaled)):
            high = values.astype(BF16)
            out_ref[m, 0, here] = high
            out_ref[m, 1, here] = (values - high.astype(F32)).astype(BF16)


def reduce_cells(step, list_ref, feat_ref, in_ref, acc_ref):
    role = unpack(list_ref[2 * step])[1]
    feat = both(feat_ref, list_ref, step)
    for m, place in enumerate((0, 1 + role)):
        acc_ref[place] += dot(feat, in_ref[m, 0]) + dot(feat, in_ref[m, 1])


def pair_body(at, place_ref, count_ref, scale_ref, own_ref, rows_ref, left_ref, feat_ref, right_ref, out_ref, acc_ref, kernel_ref, list_ref, *stages):
    product_refs, weight_refs = stages[:2], stages[2:]
    mine = own_block(place_ref[0, 0], at)
    steps = list_cells(mine, count_ref, list_ref)
    own = own_ref[:, pl.ds(pl.multiple_of(mine * BLOCK, BLOCK), BLOCK)]
    acc_ref[...] = jnp.zeros_like(acc_ref)
    kernel_ref[...] = jnp.zeros_like(kernel_ref)
    weight_refs[1][...] = jnp.zeros_like(weight_refs[1])
    products(1, list_ref, left_ref, right_ref, at, product_refs[0])

    def visit(i, carry):
        for u in range(2):
            now, later, step = u, 1 - u, 2 * i + u
            reduce_cells(step, list_ref, feat_ref, weight_refs[later], acc_ref)
            weights(step + 1, list_ref, rows_ref, product_refs[now], weight_refs[now], kernel_ref)
            products(step + 2, list_ref, left_ref, right_ref, at, product_refs[later])
        return carry

    rounds = (steps + 1) // 2
    lax.fori_loop(0, rounds, visit, 0)
    reduce_cells(2 * rounds, list_ref, feat_ref, weight_refs[1], acc_ref)

    scale = scale_ref[0, 0]
    pushing, target, source = (acc_ref[m, 0:8] + acc_ref[m, 8:16] + acc_ref[m, 16:24] for m in range(3))
    center, normal = own[0:3], own[3:6]
    weight = scale * own[6:7]
    push = center * pushing[6:7] - pushing[0:3]
    pull = normal * target[6:7] + source[3:6]
    out_ref[0:3, :] = weight * (2.0 * pull - 4.0 * push)
    out_ref[3:6, :] = 2.0 * weight * (center * target[6:7] - target[0:3])
    out_ref[6:7, :] = scale * jnp.sum(kernel_ref[...], axis=0, keepdims=True)
    out_ref[7:8, :] = jnp.zeros((1, BLOCK), F32)


def outer_kernel(*refs):
    place_ref, (out_ref, edge_ref), scratch = refs[0], refs[8:10], refs[10:]
    pair_body(0, *refs[:8], out_ref, *scratch)
    core = place_ref[0, 0]
    gap = jnp.zeros((1, HALO_FACES), F32)
    tails, heads = [], []
    for c in range(3):
        tails += [out_ref[c : c + 1, BLOCK - HALO_FACES :], gap]
        heads += [gap, out_ref[c : c + 1, :HALO_FACES]]
    rest = [gap] * (2 * BLOCK // HALO_FACES - 6)
    edge_ref[...] = jnp.where(core == 0, jnp.concatenate(tails + rest, axis=1), jnp.concatenate(heads + rest, axis=1))


def inner_kernel(*refs):
    pair_body(1, *refs)


def pair_call(body, outputs, operands, name):
    partners = operands[1].shape[1] // 2
    cells = partners // 3
    in_specs = [SMEM] * 3 + [VMEM] * (len(operands) - 3)
    return pl.pallas_call(
        body,
        out_shape=outputs,
        in_specs=in_specs,
        out_specs=jax.tree.map(lambda _: VMEM, outputs),
        scratch_shapes=[
            pltpu.VMEM((3, 32, BLOCK), F32),
            pltpu.VMEM((8, BLOCK), F32),
            pltpu.SMEM((2 * partners + 16,), jnp.int32),
        ]
        + [pltpu.VMEM((2, 2 * SLICE, BLOCK), F32)] * 2
        + [pltpu.VMEM((2, 2, 2 * SLICE, BLOCK), BF16)] * 2,
        compiler_params=pltpu.CompilerParams(vmem_limit_bytes=24 * 1024 * 1024),
        cost_estimate=pl.CostEstimate(
            flops=cells * BLOCK * BLOCK * 500, bytes_accessed=1 << 21, transcendentals=cells * BLOCK * BLOCK
        ),
        name=name,
    )(*operands)


def incidence_kernel(corner_ref, out_ref):
    verts, faces = out_ref.shape
    vertex = lax.broadcasted_iota(jnp.int32, (verts, 128), 0)
    for e in range(0, faces, 128):
        total = jnp.zeros((verts, 128), F32)
        for k in range(3):
            total = total + jnp.where(corner_ref[k : k + 1, e : e + 128] == vertex, 1.0, 0.0)
        out_ref[:, e : e + 128] = total.astype(BF16)


def incidence_table(corner, verts):
    faces = corner.shape[1]
    return pl.pallas_call(
        incidence_kernel,
        out_shape=jax.ShapeDtypeStruct((verts, faces), BF16),
        in_specs=[VMEM],
        out_specs=VMEM,
        compiler_params=pltpu.CompilerParams(vmem_limit_bytes=16 * 1024 * 1024),
        cost_estimate=pl.CostEstimate(flops=verts * faces * 9, bytes_accessed=verts * faces * 2, transcendentals=0),
        name="incidence",
    )(corner)


def finish_kernel(parts_ref, table_ref, vertex_ref, face_ref):
    sums = []
    for core in range(2):
        total = parts_ref[core]
        for i in range(core + 2, parts_ref.shape[0], 2):
            total = total + parts_ref[i]
        sums.append(total)
    low, high = sums[1], sums[0]
    total = jnp.concatenate([low[:, :BLOCK], low[:, BLOCK:], high[:, BLOCK:], high[:, :BLOCK]], axis=1)
    faces = total.shape[1]
    width = 2 * HALO_FACES
    face_ref[...] = total[3:7]
    edges = low[7:8] + high[7:8]
    edge = jnp.concatenate([edges[:, c * width : (c + 1) * width] for c in range(3)], axis=0)
    contract = (((1,), (1,)), ((), ()))
    out = jnp.zeros((3, vertex_ref.shape[1]), F32)
    for main, side in zip(thirds(total[0:3]), thirds(edge)):
        out = out + lax.dot_general(main.astype(BF16), table_ref[:, 0:faces], contract, preferred_element_type=F32)
        out = out + lax.dot_general(side.astype(BF16), table_ref[:, faces:], contract, preferred_element_type=F32)
    vertex_ref[...] = out / 3.0


def finish(parts, table):
    verts, faces = table.shape[0], 2 * parts.shape[2]
    return pl.pallas_call(
        finish_kernel,
        out_shape=(jax.ShapeDtypeStruct((3, verts), F32), jax.ShapeDtypeStruct((4, faces), F32)),
        in_specs=[VMEM, VMEM],
        out_specs=(VMEM, VMEM),
        compiler_params=pltpu.CompilerParams(vmem_limit_bytes=16 * 1024 * 1024),
        name="finish",
    )(parts, table)


def shards(centroids, normals, areas, cotangent, pair_code, corner_vertex):
    count, shares = lax.axis_size("blk"), lax.axis_size("pair")
    faces = centroids.shape[1]
    assert shares // 2 * SLICE == faces
    member = lax.axis_index("pair")
    core, slab = member % 2, member // 2
    other_block = slab * SLICE // BLOCK

    own = jnp.concatenate([centroids, normals, areas[None], jnp.zeros((1, faces), F32)], axis=0)
    codes = pair_code.reshape(count)
    piece = lax.dynamic_slice_in_dim(own, slab * SLICE, SLICE, axis=1)
    line = lax.broadcasted_iota(jnp.int32, (1, 8, SLICE), 1)
    chunks = jnp.where(line == 7, codes.astype(F32)[:, None, None], piece[None])
    rows = lax.all_to_all(chunks, "blk", 0, 0)

    incoming = rows[:, 7, 0].astype(jnp.int32)
    pack = jnp.concatenate([incoming, codes]).reshape(1, 1, 2 * count)
    held = lax.all_to_all(jnp.broadcast_to(pack, (shares, 1, 2 * count)), "pair", 0, 0)
    place = jnp.stack([core, other_block]).reshape(1, 2)
    counts = tally(place, held)
    scale = cotangent.reshape(1, 1)
    corner = jnp.concatenate(
        [corner_vertex[:, HALO_FACES:-HALO_FACES], corner_vertex[:, :HALO_FACES], corner_vertex[:, -HALO_FACES:]], axis=1
    )
    table = incidence_table(corner, faces // 2)

    block = jax.ShapeDtypeStruct((8, BLOCK), F32)
    edge_row = jax.ShapeDtypeStruct((1, 2 * BLOCK), F32)
    operands = (place, counts, scale, own, rows, *features(place, own, rows))
    outer, edge = pair_call(outer_kernel, (block, edge_row), operands, "outer_block")

    def neighbour(b, member):
        return (b + (1 if member % 2 == 0 else count - 1)) % count * shares + member

    hops = [(b * shares + m, neighbour(b, m)) for b in range(count) for m in range(shares)]
    halo = lax.ppermute(edge, ("blk", "pair"), hops)
    inner = pair_call(inner_kernel, block, operands, "inner_block")
    part = jnp.concatenate([jnp.concatenate([outer, inner], axis=1)[:7], halo], axis=0)
    parts = lax.all_gather(part, "pair")
    return finish(parts, table)


def solution(mesh):
    placed = (
        P(None, "blk"),
        P(None, "blk"),
        P("blk"),
        P(),
        P("blk", "pair", None, None),
        P(None, "blk"),
    )
    return jax.shard_map(
        shards,
        mesh=mesh,
        in_specs=placed,
        out_specs=(P(None, "blk"), P(None, "blk")),
        check_vma=False,
    )
```

```python
import functools

import jax
import jax.numpy as jnp
from jax import lax
from jax.experimental import pallas as pl
from jax.experimental.pallas import tpu as pltpu
from jax.sharding import PartitionSpec as P

BLOCK = 256
FB_DEV = 4
HALO_FACES = 64
CODES = FB_DEV * FB_DEV
DEPTH = 64
SLICE = 128
LEFT = (0, 0, 1, 1, 0, 2)
RIGHT = (0, 1, 0, 1, 2, 0)
ONES = (0, 1, 4)
F32 = jnp.float32
BF16 = jnp.bfloat16
VMEM = pl.BlockSpec(memory_space=pltpu.VMEM)
SMEM = pl.BlockSpec(memory_space=pltpu.SMEM)
dot = functools.partial(jnp.dot, preferred_element_type=F32)


def thirds(values):
    high = values.astype(BF16).astype(F32)
    rest = values - high
    middle = rest.astype(BF16).astype(F32)
    return [high, middle, (rest - middle).astype(BF16).astype(F32)]


def square(x):
    return jnp.sum(x[0:3] * x[0:3], axis=0, keepdims=True)


def lever(x):
    return jnp.sum(x[0:3] * x[3:6], axis=0, keepdims=True)


def partner_features(rows, left_ref, feat_ref, base):
    x = jnp.concatenate(rows, axis=1)
    width = x.shape[1]
    row = lax.broadcasted_iota(jnp.int32, x.shape, 0)
    area = x[6:7]
    x = jnp.where(row >= 6, 1.0, x)
    split = thirds(x)
    extra = thirds(square(x)) + thirds(lever(x)) + [jnp.zeros((10, width), F32)]
    left = jnp.concatenate([split[i] for i in LEFT] + extra, axis=0).astype(BF16)
    feat = jnp.concatenate(thirds(x * area) + [jnp.zeros((8, width), F32)], axis=0).astype(BF16)
    for i in range(len(rows)):
        columns = slice(i * SLICE, (i + 1) * SLICE)
        left_ref[base + i] = left[:, columns]
        feat_ref[base + i] = feat[:, columns]


def own_features(x, right_ref, at):
    row = lax.broadcasted_iota(jnp.int32, (8, BLOCK), 0)
    zero = jnp.zeros((8, BLOCK), F32)
    first, second = row < 3, jnp.logical_and(row >= 3, row < 6)
    center = thirds(-2.0 * x)
    swapped = thirds(jnp.concatenate([x[3:6], x[0:3], x[6:8]], axis=0))
    distance, level = thirds(square(x) + 1.0), thirds(lever(x))
    sides = (
        [jnp.where(first, center[i], zero) for i in RIGHT],
        [jnp.where(first, -swapped[i], zero) for i in RIGHT],
        [jnp.where(second, swapped[i], zero) for i in RIGHT],
    )
    for i, g in enumerate(ONES):
        sides[0][g] = jnp.where(row == 7, distance[i], sides[0][g])
        sides[1][g] = jnp.where(row == 7, level[i], sides[1][g])
    tails = (jnp.where(first, 1.0, zero), zero, jnp.where(second, -1.0, zero))
    for m in range(3):
        right_ref[at, m] = jnp.concatenate(sides[m] + [tails[m], zero], axis=0).astype(BF16)


def own_block(core, at):
    return jnp.where(core == 0, FB_DEV - 1 - at, at)


def feature_kernel(place_ref, own_ref, rows_ref, left_ref, feat_ref, right_ref):
    for at in range(2):
        first = pl.multiple_of(own_block(place_ref[0, 0], at) * BLOCK, BLOCK)
        own_features(own_ref[:, pl.ds(first, BLOCK)], right_ref, at)
    for k in range(0, rows_ref.shape[0], 8):
        partner_features([rows_ref[k + i] for i in range(8)], left_ref, feat_ref, k)


def features(place, own, rows):
    n = rows.shape[0]
    return pl.pallas_call(
        feature_kernel,
        out_shape=(
            jax.ShapeDtypeStruct((n, DEPTH, SLICE), BF16),
            jax.ShapeDtypeStruct((n, 32, SLICE), BF16),
            jax.ShapeDtypeStruct((2, 3, DEPTH, BLOCK), BF16),
        ),
        in_specs=[SMEM, VMEM, VMEM],
        out_specs=(VMEM, VMEM, VMEM),
        compiler_params=pltpu.CompilerParams(vmem_limit_bytes=16 * 1024 * 1024),
        cost_estimate=pl.CostEstimate(flops=1 << 22, bytes_accessed=1 << 20, transcendentals=0),
        name="features",
    )(place, own, rows)


def tally_kernel(place_ref, held_ref, out_ref):
    other = place_ref[0, 1]
    held = held_ref[...]
    lanes = held.shape[2]
    half = lanes // 2
    lane = lax.broadcasted_iota(jnp.int32, (1, lanes), 1)
    rows = []
    for o in range(FB_DEV):
        code = jnp.where(lane < half, o * FB_DEV + other, other * FB_DEV + o)
        rows.append(jnp.sum(jnp.where(held == code[None], 1.0, 0.0), axis=0))
    counts = jnp.concatenate(rows + [jnp.zeros((8 - FB_DEV, lanes), F32)], axis=0).T
    active = counts > 0.0
    at, before = (lax.broadcasted_iota(jnp.int32, (lanes, lanes), i) for i in range(2))
    upto = jnp.logical_and(before <= at, (before < half) == (at < half))
    order = dot(jnp.where(upto, 1.0, 0.0).astype(BF16), jnp.where(active, 1.0, 0.0).astype(BF16)).astype(jnp.int32)
    place = jnp.where(active, order - 1, -1)
    index = lax.broadcasted_iota(jnp.int32, counts.shape, 0) % half
    value = counts.astype(jnp.int32) * 256 + index
    slot = lax.broadcasted_iota(jnp.int32, (half, 128), 1)
    for o in range(FB_DEV):
        for role in range(2):
            mine = slice(role * half, (role + 1) * half)
            hit = slot == place[mine, o : o + 1]
            entries = jnp.sum(jnp.where(hit, value[mine, o : o + 1].astype(F32), 0.0), axis=0, keepdims=True)
            total = order[(role + 1) * half - 1 : (role + 1) * half, o : o + 1].astype(F32)
            entries = jnp.where(slot[0:1] == 127, total, entries)
            out_ref[o : o + 1, role * 128 : (role + 1) * 128] = entries.astype(jnp.int32)


def tally(place, held):
    return pl.pallas_call(
        tally_kernel,
        out_shape=jax.ShapeDtypeStruct((FB_DEV, 256), jnp.int32),
        in_specs=[SMEM, VMEM],
        out_specs=VMEM,
        compiler_params=pltpu.CompilerParams(vmem_limit_bytes=16 * 1024 * 1024),
        name="tally",
    )(place, held)


def prepare_kernel(place_ref, code_ref, center_ref, normal_ref, area_ref, own_ref, chunk_ref):
    own_ref[0:3, :] = center_ref[...]
    own_ref[3:6, :] = normal_ref[...]
    own_ref[6:7, :] = area_ref[...]
    own_ref[7:8, :] = jnp.zeros_like(area_ref)
    piece = own_ref[:, pl.ds(pl.multiple_of(place_ref[0, 2] * SLICE, SLICE), SLICE)]
    last = lax.broadcasted_iota(jnp.int32, piece.shape, 0) == 7
    for b in range(chunk_ref.shape[0]):
        chunk_ref[b] = jnp.where(last, code_ref[0, b].astype(F32), piece)


def prepare(place, codes, centroids, normals, areas):
    count, faces = codes.shape[1], centroids.shape[1]
    return pl.pallas_call(
        prepare_kernel,
        out_shape=(jax.ShapeDtypeStruct((8, faces), F32), jax.ShapeDtypeStruct((count, 8, SLICE), F32)),
        in_specs=[SMEM, SMEM, VMEM, VMEM, VMEM],
        out_specs=(VMEM, VMEM),
        compiler_params=pltpu.CompilerParams(vmem_limit_bytes=16 * 1024 * 1024),
        name="prepare",
    )(place, codes, centroids, normals, areas)


def pack_kernel(code_ref, rows_ref, out_ref):
    values = rows_ref[:, 7, :]
    count = values.shape[0]
    lane, row = (lax.broadcasted_iota(jnp.int32, values.shape, i) for i in (1, 0))
    incoming = jnp.sum(jnp.where(lane == row, values, 0.0), axis=0, keepdims=True)
    both_ways = jnp.concatenate([incoming[:, :count], code_ref[...].astype(F32)], axis=1).astype(jnp.int32)
    out_ref[...] = jnp.broadcast_to(both_ways[None], out_ref.shape)


def pack_codes(codes, rows, shares):
    return pl.pallas_call(
        pack_kernel,
        out_shape=jax.ShapeDtypeStruct((shares, 1, 2 * codes.shape[1]), jnp.int32),
        in_specs=[VMEM, VMEM],
        out_specs=VMEM,
        compiler_params=pltpu.CompilerParams(vmem_limit_bytes=16 * 1024 * 1024),
        name="pack_codes",
    )(codes, rows)


class Steps:
    def __init__(self, mine, list_ref):
        self.mine, self.list_ref = mine, list_ref
        self.first = (list_ref[mine, 127] + 1) // 2
        self.number = self.first + (list_ref[mine, 255] + 1) // 2

    def role(self, step):
        return (step >= self.first).astype(jnp.int32)

    def entry(self, step, h):
        role = self.role(step)
        entry = self.list_ref[self.mine, role * 128 + 2 * (step - role * self.first) + h]
        return entry // 256, entry % 256

    def beside(self, step, ref):
        return jnp.concatenate([ref[self.entry(step, h)[1]] for h in range(2)], axis=1)


def products(step, steps, left_ref, right_ref, at, out_ref):
    left = steps.beside(step, left_ref)
    over = (((0,), (0,)), ((), ()))
    out_ref[0] = lax.dot_general(left, right_ref[at, 0], over, preferred_element_type=F32)
    out_ref[1] = lax.dot_general(left, right_ref[at, 1 + steps.role(step)], over, preferred_element_type=F32)


def weights(step, steps, rows_ref, in_ref, out_ref, kernel_ref):
    for h in range(2):
        count, x = steps.entry(step, h)
        area = rows_ref[x].T[:, 6:7]
        here = slice(h * SLICE, (h + 1) * SLICE)
        inverse = pl.reciprocal(in_ref[0, here], approx=True)
        projected = in_ref[1, here]
        scaled = inverse * inverse * count.astype(F32)
        kernel = (projected * projected + 1.0) * scaled
        kernel_ref[...] += jnp.sum((kernel * area).reshape(SLICE // 8, 8, BLOCK), axis=0)
        for m, values in enumerate((kernel * inverse, projected * scaled)):
            high = values.astype(BF16)
            out_ref[m, 0, here] = high
            out_ref[m, 1, here] = (values - high.astype(F32)).astype(BF16)


def reduce_cells(step, steps, feat_ref, in_ref, acc_ref):
    feat = steps.beside(step, feat_ref)
    for m, place in enumerate((0, 1 + steps.role(step))):
        acc_ref[place] += dot(feat, in_ref[m, 0]) + dot(feat, in_ref[m, 1])


def pair_body(at, place_ref, list_ref, scale_ref, own_ref, rows_ref, left_ref, feat_ref, right_ref, out_ref, acc_ref, kernel_ref, *stages):
    product_refs, weight_refs = stages[:2], stages[2:]
    mine = own_block(place_ref[0, 0], at)
    steps = Steps(mine, list_ref)
    own = own_ref[:, pl.ds(pl.multiple_of(mine * BLOCK, BLOCK), BLOCK)]
    acc_ref[...] = jnp.zeros_like(acc_ref)
    kernel_ref[...] = jnp.zeros_like(kernel_ref)
    weight_refs[1][...] = jnp.zeros_like(weight_refs[1])
    products(0, steps, left_ref, right_ref, at, product_refs[0])

    def visit(i, carry):
        for u in range(2):
            now, later, step = u, 1 - u, 2 * i + u
            reduce_cells(jnp.maximum(step - 1, 0), steps, feat_ref, weight_refs[later], acc_ref)
            weights(step, steps, rows_ref, product_refs[now], weight_refs[now], kernel_ref)
            products(step + 1, steps, left_ref, right_ref, at, product_refs[later])
        return carry

    rounds = (steps.number + 1) // 2
    lax.fori_loop(0, rounds, visit, 0)
    reduce_cells(jnp.maximum(2 * rounds - 1, 0), steps, feat_ref, weight_refs[1], acc_ref)

    scale = scale_ref[0, 0]
    pushing, target, source = (acc_ref[m, 0:8] + acc_ref[m, 8:16] + acc_ref[m, 16:24] for m in range(3))
    center, normal = own[0:3], own[3:6]
    weight = scale * own[6:7]
    push = center * pushing[6:7] - pushing[0:3]
    pull = normal * target[6:7] + source[3:6]
    out_ref[0:3, :] = weight * (2.0 * pull - 4.0 * push)
    out_ref[3:6, :] = 2.0 * weight * (center * target[6:7] - target[0:3])
    out_ref[6:7, :] = scale * jnp.sum(kernel_ref[...], axis=0, keepdims=True)
    out_ref[7:8, :] = jnp.zeros((1, BLOCK), F32)


def outer_kernel(*refs):
    place_ref, (out_ref, edge_ref), scratch = refs[0], refs[8:10], refs[10:]
    pair_body(0, *refs[:8], out_ref, *scratch)
    core = place_ref[0, 0]
    gap = jnp.zeros((1, HALO_FACES), F32)
    tails, heads = [], []
    for c in range(3):
        tails += [out_ref[c : c + 1, BLOCK - HALO_FACES :], gap]
        heads += [gap, out_ref[c : c + 1, :HALO_FACES]]
    rest = [gap] * (2 * BLOCK // HALO_FACES - 6)
    edge_ref[...] = jnp.where(core == 0, jnp.concatenate(tails + rest, axis=1), jnp.concatenate(heads + rest, axis=1))


def inner_kernel(*refs):
    pair_body(1, *refs)


def pair_call(body, outputs, operands, name):
    cells = operands[4].shape[0] // 3
    in_specs = [SMEM] * 3 + [VMEM] * (len(operands) - 3)
    return pl.pallas_call(
        body,
        out_shape=outputs,
        in_specs=in_specs,
        out_specs=jax.tree.map(lambda _: VMEM, outputs),
        scratch_shapes=[
            pltpu.VMEM((3, 32, BLOCK), F32),
            pltpu.VMEM((8, BLOCK), F32),
        ]
        + [pltpu.VMEM((2, 2 * SLICE, BLOCK), F32)] * 2
        + [pltpu.VMEM((2, 2, 2 * SLICE, BLOCK), BF16)] * 2,
        compiler_params=pltpu.CompilerParams(vmem_limit_bytes=24 * 1024 * 1024),
        cost_estimate=pl.CostEstimate(
            flops=cells * BLOCK * BLOCK * 500, bytes_accessed=1 << 21, transcendentals=cells * BLOCK * BLOCK
        ),
        name=name,
    )(*operands)


def incidence_kernel(corner_ref, out_ref):
    verts, faces = out_ref.shape
    vertex = lax.broadcasted_iota(jnp.int32, (verts, 128), 0)
    for e in range(0, faces, 128):
        total = jnp.zeros((verts, 128), F32)
        for k in range(3):
            total = total + jnp.where(corner_ref[k : k + 1, e : e + 128] == vertex, 1.0, 0.0)
        out_ref[:, e : e + 128] = total.astype(BF16)


def incidence_table(corner, verts):
    faces = corner.shape[1]
    return pl.pallas_call(
        incidence_kernel,
        out_shape=jax.ShapeDtypeStruct((verts, faces), BF16),
        in_specs=[VMEM],
        out_specs=VMEM,
        compiler_params=pltpu.CompilerParams(vmem_limit_bytes=16 * 1024 * 1024),
        cost_estimate=pl.CostEstimate(flops=verts * faces * 9, bytes_accessed=verts * faces * 2, transcendentals=0),
        name="incidence",
    )(corner)


def finish_kernel(parts_ref, table_ref, vertex_ref, face_ref):
    sums = []
    for core in range(2):
        total = parts_ref[core]
        for i in range(core + 2, parts_ref.shape[0], 2):
            total = total + parts_ref[i]
        sums.append(total)
    low, high = sums[1], sums[0]
    total = jnp.concatenate([low[:, :BLOCK], low[:, BLOCK:], high[:, BLOCK:], high[:, :BLOCK]], axis=1)
    faces = total.shape[1]
    width = 2 * HALO_FACES
    face_ref[...] = total[3:7]
    edges = low[7:8] + high[7:8]
    edge = jnp.concatenate([edges[:, c * width : (c + 1) * width] for c in range(3)], axis=0)
    contract = (((1,), (1,)), ((), ()))
    out = jnp.zeros((3, vertex_ref.shape[1]), F32)
    for main, side in zip(thirds(total[0:3]), thirds(edge)):
        out = out + lax.dot_general(main.astype(BF16), table_ref[:, 0:faces], contract, preferred_element_type=F32)
        out = out + lax.dot_general(side.astype(BF16), table_ref[:, faces:], contract, preferred_element_type=F32)
    vertex_ref[...] = out / 3.0


def finish(parts, table):
    verts, faces = table.shape[0], 2 * parts.shape[2]
    return pl.pallas_call(
        finish_kernel,
        out_shape=(jax.ShapeDtypeStruct((3, verts), F32), jax.ShapeDtypeStruct((4, faces), F32)),
        in_specs=[VMEM, VMEM],
        out_specs=(VMEM, VMEM),
        compiler_params=pltpu.CompilerParams(vmem_limit_bytes=16 * 1024 * 1024),
        name="finish",
    )(parts, table)


def shards(centroids, normals, areas, cotangent, pair_code, corner_vertex):
    count, shares = lax.axis_size("blk"), lax.axis_size("pair")
    faces = centroids.shape[1]
    assert shares // 2 * SLICE == faces
    member = lax.axis_index("pair")
    core, slab = member % 2, member // 2
    other_block = slab * SLICE // BLOCK

    place = jnp.stack([core, other_block, slab]).reshape(1, 3)
    codes = pair_code.transpose(0, 1, 3, 2).reshape(1, count)
    own, chunks = prepare(place, codes, centroids, normals, areas.reshape(1, faces))
    rows = lax.all_to_all(chunks, "blk", 0, 0)

    held = lax.all_to_all(pack_codes(codes, rows, shares), "pair", 0, 0)
    counts = tally(place, held)
    scale = cotangent.reshape(1, 1)
    corner = jnp.concatenate(
        [corner_vertex[:, HALO_FACES:-HALO_FACES], corner_vertex[:, :HALO_FACES], corner_vertex[:, -HALO_FACES:]], axis=1
    )
    table = incidence_table(corner, faces // 2)

    block = jax.ShapeDtypeStruct((8, BLOCK), F32)
    edge_row = jax.ShapeDtypeStruct((1, 2 * BLOCK), F32)
    operands = (place, counts, scale, own, rows, *features(place, own, rows))
    outer, edge = pair_call(outer_kernel, (block, edge_row), operands, "outer_block")

    def neighbour(b, member):
        return (b + (1 if member % 2 == 0 else count - 1)) % count * shares + member

    hops = [(b * shares + m, neighbour(b, m)) for b in range(count) for m in range(shares)]
    halo = lax.ppermute(edge, ("blk", "pair"), hops)
    inner = pair_call(inner_kernel, block, operands, "inner_block")
    part = jnp.concatenate([jnp.concatenate([outer, inner], axis=1)[:7], halo], axis=0)
    parts = lax.all_to_all(jnp.broadcast_to(part[None], (shares, *part.shape)), "pair", 0, 0)
    return finish(parts, table)


def solution(mesh):
    placed = (
        P(None, "blk"),
        P(None, "blk"),
        P("blk"),
        P(),
        P("blk", "pair", None, None),
        P(None, "blk"),
    )
    return jax.shard_map(
        shards,
        mesh=mesh,
        in_specs=placed,
        out_specs=(P(None, "blk"), P(None, "blk")),
        check_vma=False,
    )
```

```python
import functools

import jax
import jax.numpy as jnp
from jax import lax
from jax.experimental import pallas as pl
from jax.experimental.pallas import tpu as pltpu
from jax.sharding import PartitionSpec as P

BLOCK = 256
FB_DEV = 4
HALO_FACES = 64
CODES = FB_DEV * FB_DEV
DEPTH = 64
SLICE = 128
LEFT = (0, 0, 1, 1, 0, 2)
RIGHT = (0, 1, 0, 1, 2, 0)
ONES = (0, 1, 4)
F32 = jnp.float32
BF16 = jnp.bfloat16
VMEM = pl.BlockSpec(memory_space=pltpu.VMEM)
SMEM = pl.BlockSpec(memory_space=pltpu.SMEM)
dot = functools.partial(jnp.dot, preferred_element_type=F32)


def thirds(values):
    high = values.astype(BF16).astype(F32)
    rest = values - high
    middle = rest.astype(BF16).astype(F32)
    return [high, middle, (rest - middle).astype(BF16).astype(F32)]


def square(x):
    return jnp.sum(x[0:3] * x[0:3], axis=0, keepdims=True)


def lever(x):
    return jnp.sum(x[0:3] * x[3:6], axis=0, keepdims=True)


def partner_features(rows, left_ref, feat_ref, base):
    x = jnp.concatenate(rows, axis=1)
    width = x.shape[1]
    row = lax.broadcasted_iota(jnp.int32, x.shape, 0)
    area = x[6:7]
    x = jnp.where(row >= 6, 1.0, x)
    split = thirds(x)
    extra = thirds(square(x)) + thirds(lever(x)) + [jnp.zeros((10, width), F32)]
    left = jnp.concatenate([split[i] for i in LEFT] + extra, axis=0).astype(BF16)
    feat = jnp.concatenate(thirds(x * area) + [jnp.zeros((8, width), F32)], axis=0).astype(BF16)
    for i in range(len(rows)):
        columns = slice(i * SLICE, (i + 1) * SLICE)
        left_ref[base + i] = left[:, columns]
        feat_ref[base + i] = feat[:, columns]


def own_features(x, right_ref, at):
    row = lax.broadcasted_iota(jnp.int32, (8, BLOCK), 0)
    zero = jnp.zeros((8, BLOCK), F32)
    first, second = row < 3, jnp.logical_and(row >= 3, row < 6)
    center = thirds(-2.0 * x)
    swapped = thirds(jnp.concatenate([x[3:6], x[0:3], x[6:8]], axis=0))
    distance, level = thirds(square(x) + 1.0), thirds(lever(x))
    sides = (
        [jnp.where(first, center[i], zero) for i in RIGHT],
        [jnp.where(first, -swapped[i], zero) for i in RIGHT],
        [jnp.where(second, swapped[i], zero) for i in RIGHT],
    )
    for i, g in enumerate(ONES):
        sides[0][g] = jnp.where(row == 7, distance[i], sides[0][g])
        sides[1][g] = jnp.where(row == 7, level[i], sides[1][g])
    tails = (jnp.where(first, 1.0, zero), zero, jnp.where(second, -1.0, zero))
    for m in range(3):
        right_ref[at, m] = jnp.concatenate(sides[m] + [tails[m], zero], axis=0).astype(BF16)


def own_block(core, at):
    return jnp.where(core == 0, FB_DEV - 1 - at, at)


def feature_kernel(place_ref, own_ref, rows_ref, left_ref, feat_ref, right_ref):
    for at in range(2):
        first = pl.multiple_of(own_block(place_ref[0, 0], at) * BLOCK, BLOCK)
        own_features(own_ref[:, pl.ds(first, BLOCK)], right_ref, at)
    for k in range(0, rows_ref.shape[0], 8):
        partner_features([rows_ref[k + i] for i in range(8)], left_ref, feat_ref, k)


def features(place, own, rows):
    n = rows.shape[0]
    return pl.pallas_call(
        feature_kernel,
        out_shape=(
            jax.ShapeDtypeStruct((n, DEPTH, SLICE), BF16),
            jax.ShapeDtypeStruct((n, 32, SLICE), BF16),
            jax.ShapeDtypeStruct((2, 3, DEPTH, BLOCK), BF16),
        ),
        in_specs=[SMEM, VMEM, VMEM],
        out_specs=(VMEM, VMEM, VMEM),
        compiler_params=pltpu.CompilerParams(vmem_limit_bytes=16 * 1024 * 1024),
        cost_estimate=pl.CostEstimate(flops=1 << 22, bytes_accessed=1 << 20, transcendentals=0),
        name="features",
    )(place, own, rows)


def tally_kernel(place_ref, held_ref, out_ref):
    other = place_ref[0, 1]
    held = held_ref[...]
    lanes = held.shape[2]
    half = lanes // 2
    lane = lax.broadcasted_iota(jnp.int32, (1, lanes), 1)
    rows = []
    for o in range(FB_DEV):
        code = jnp.where(lane < half, o * FB_DEV + other, other * FB_DEV + o)
        rows.append(jnp.sum(jnp.where(held == code[None], 1.0, 0.0), axis=0))
    counts = jnp.concatenate(rows + [jnp.zeros((8 - FB_DEV, lanes), F32)], axis=0).T
    active = counts > 0.0
    at, before = (lax.broadcasted_iota(jnp.int32, (lanes, lanes), i) for i in range(2))
    upto = jnp.logical_and(before <= at, (before < half) == (at < half))
    order = dot(jnp.where(upto, 1.0, 0.0).astype(BF16), jnp.where(active, 1.0, 0.0).astype(BF16)).astype(jnp.int32)
    place = jnp.where(active, order - 1, -1)
    index = lax.broadcasted_iota(jnp.int32, counts.shape, 0) % half
    value = counts.astype(jnp.int32) * 256 + index
    slot = lax.broadcasted_iota(jnp.int32, (half, 128), 1)
    for o in range(FB_DEV):
        for role in range(2):
            mine = slice(role * half, (role + 1) * half)
            hit = slot == place[mine, o : o + 1]
            entries = jnp.sum(jnp.where(hit, value[mine, o : o + 1].astype(F32), 0.0), axis=0, keepdims=True)
            total = order[(role + 1) * half - 1 : (role + 1) * half, o : o + 1].astype(F32)
            entries = jnp.where(slot[0:1] == 127, total, entries)
            out_ref[o : o + 1, role * 128 : (role + 1) * 128] = entries.astype(jnp.int32)


def tally(place, held):
    return pl.pallas_call(
        tally_kernel,
        out_shape=jax.ShapeDtypeStruct((FB_DEV, 256), jnp.int32),
        in_specs=[SMEM, VMEM],
        out_specs=VMEM,
        compiler_params=pltpu.CompilerParams(vmem_limit_bytes=16 * 1024 * 1024),
        name="tally",
    )(place, held)


def prepare_kernel(place_ref, code_ref, center_ref, normal_ref, area_ref, own_ref, chunk_ref):
    own_ref[0:3, :] = center_ref[...]
    own_ref[3:6, :] = normal_ref[...]
    own_ref[6:7, :] = area_ref[...]
    own_ref[7:8, :] = jnp.zeros_like(area_ref)
    piece = own_ref[:, pl.ds(pl.multiple_of(place_ref[0, 2] * SLICE, SLICE), SLICE)]
    last = lax.broadcasted_iota(jnp.int32, piece.shape, 0) == 7
    for b in range(chunk_ref.shape[0]):
        chunk_ref[b] = jnp.where(last, code_ref[0, b].astype(F32), piece)


def prepare(place, codes, centroids, normals, areas):
    count, faces = codes.shape[1], centroids.shape[1]
    return pl.pallas_call(
        prepare_kernel,
        out_shape=(jax.ShapeDtypeStruct((8, faces), F32), jax.ShapeDtypeStruct((count, 8, SLICE), F32)),
        in_specs=[SMEM, SMEM, VMEM, VMEM, VMEM],
        out_specs=(VMEM, VMEM),
        compiler_params=pltpu.CompilerParams(vmem_limit_bytes=60 * 1024 * 1024),
        name="prepare",
    )(place, codes, centroids, normals, areas)


def pack_kernel(code_ref, rows_ref, out_ref):
    values = rows_ref[:, 7, :]
    count = values.shape[0]
    lane, row = (lax.broadcasted_iota(jnp.int32, values.shape, i) for i in (1, 0))
    incoming = jnp.sum(jnp.where(lane == row, values, 0.0), axis=0, keepdims=True)
    both_ways = jnp.concatenate([incoming[:, :count], code_ref[...].astype(F32)], axis=1).astype(jnp.int32)
    out_ref[...] = jnp.broadcast_to(both_ways[None], out_ref.shape)


def pack_codes(codes, rows, shares):
    return pl.pallas_call(
        pack_kernel,
        out_shape=jax.ShapeDtypeStruct((shares, 1, 2 * codes.shape[1]), jnp.int32),
        in_specs=[VMEM, VMEM],
        out_specs=VMEM,
        compiler_params=pltpu.CompilerParams(vmem_limit_bytes=16 * 1024 * 1024),
        name="pack_codes",
    )(codes, rows)


class Steps:
    def __init__(self, mine, list_ref):
        self.mine, self.list_ref = mine, list_ref
        self.first = (list_ref[mine, 127] + 1) // 2
        self.number = self.first + (list_ref[mine, 255] + 1) // 2

    def role(self, step):
        return (step >= self.first).astype(jnp.int32)

    def entry(self, step, h):
        role = self.role(step)
        entry = self.list_ref[self.mine, role * 128 + 2 * (step - role * self.first) + h]
        return entry // 256, entry % 256

    def beside(self, step, ref):
        return jnp.concatenate([ref[self.entry(step, h)[1]] for h in range(2)], axis=1)


def products(step, steps, left_ref, right_ref, at, out_ref):
    left = steps.beside(step, left_ref)
    over = (((0,), (0,)), ((), ()))
    out_ref[0] = lax.dot_general(left, right_ref[at, 0], over, preferred_element_type=F32)
    out_ref[1] = lax.dot_general(left, right_ref[at, 1 + steps.role(step)], over, preferred_element_type=F32)


def weights(step, steps, rows_ref, in_ref, out_ref, kernel_ref):
    for h in range(2):
        count, x = steps.entry(step, h)
        area = rows_ref[x].T[:, 6:7]
        here = slice(h * SLICE, (h + 1) * SLICE)
        inverse = pl.reciprocal(in_ref[0, here], approx=True)
        projected = in_ref[1, here]
        scaled = inverse * inverse * count.astype(F32)
        kernel = (projected * projected + 1.0) * scaled
        kernel_ref[...] += jnp.sum((kernel * area).reshape(SLICE // 8, 8, BLOCK), axis=0)
        for m, values in enumerate((kernel * inverse, projected * scaled)):
            high = values.astype(BF16)
            out_ref[m, 0, here] = high
            out_ref[m, 1, here] = (values - high.astype(F32)).astype(BF16)


def reduce_cells(step, steps, feat_ref, in_ref, acc_ref):
    feat = steps.beside(step, feat_ref)
    for m, place in enumerate((0, 1 + steps.role(step))):
        acc_ref[place] += dot(feat, in_ref[m, 0]) + dot(feat, in_ref[m, 1])


def pair_body(at, place_ref, list_ref, scale_ref, own_ref, rows_ref, left_ref, feat_ref, right_ref, out_ref, acc_ref, kernel_ref, *stages):
    product_refs, weight_refs = stages[:2], stages[2:]
    mine = own_block(place_ref[0, 0], at)
    steps = Steps(mine, list_ref)
    own = own_ref[:, pl.ds(pl.multiple_of(mine * BLOCK, BLOCK), BLOCK)]
    acc_ref[...] = jnp.zeros_like(acc_ref)
    kernel_ref[...] = jnp.zeros_like(kernel_ref)
    weight_refs[1][...] = jnp.zeros_like(weight_refs[1])
    products(0, steps, left_ref, right_ref, at, product_refs[0])

    def visit(i, carry):
        for u in range(2):
            now, later, step = u, 1 - u, 2 * i + u
            reduce_cells(jnp.maximum(step - 1, 0), steps, feat_ref, weight_refs[later], acc_ref)
            weights(step, steps, rows_ref, product_refs[now], weight_refs[now], kernel_ref)
            products(step + 1, steps, left_ref, right_ref, at, product_refs[later])
        return carry

    rounds = (steps.number + 1) // 2
    lax.fori_loop(0, rounds, visit, 0)
    reduce_cells(jnp.maximum(2 * rounds - 1, 0), steps, feat_ref, weight_refs[1], acc_ref)

    scale = scale_ref[0, 0]
    pushing, target, source = (acc_ref[m, 0:8] + acc_ref[m, 8:16] + acc_ref[m, 16:24] for m in range(3))
    center, normal = own[0:3], own[3:6]
    weight = scale * own[6:7]
    push = center * pushing[6:7] - pushing[0:3]
    pull = normal * target[6:7] + source[3:6]
    out_ref[0:3, :] = weight * (2.0 * pull - 4.0 * push)
    out_ref[3:6, :] = 2.0 * weight * (center * target[6:7] - target[0:3])
    out_ref[6:7, :] = scale * jnp.sum(kernel_ref[...], axis=0, keepdims=True)
    out_ref[7:8, :] = jnp.zeros((1, BLOCK), F32)


def outer_kernel(*refs):
    place_ref, (out_ref, edge_ref), scratch = refs[0], refs[8:10], refs[10:]
    pair_body(0, *refs[:8], out_ref, *scratch)
    core = place_ref[0, 0]
    gap = jnp.zeros((1, HALO_FACES), F32)
    tails, heads = [], []
    for c in range(3):
        tails += [out_ref[c : c + 1, BLOCK - HALO_FACES :], gap]
        heads += [gap, out_ref[c : c + 1, :HALO_FACES]]
    rest = [gap] * (2 * BLOCK // HALO_FACES - 6)
    edge_ref[...] = jnp.where(core == 0, jnp.concatenate(tails + rest, axis=1), jnp.concatenate(heads + rest, axis=1))


def inner_kernel(*refs):
    pair_body(1, *refs)


def pair_call(body, outputs, operands, name):
    cells = operands[4].shape[0] // 3
    in_specs = [SMEM] * 3 + [VMEM] * (len(operands) - 3)
    return pl.pallas_call(
        body,
        out_shape=outputs,
        in_specs=in_specs,
        out_specs=jax.tree.map(lambda _: VMEM, outputs),
        scratch_shapes=[
            pltpu.VMEM((3, 32, BLOCK), F32),
            pltpu.VMEM((8, BLOCK), F32),
        ]
        + [pltpu.VMEM((2, 2 * SLICE, BLOCK), F32)] * 2
        + [pltpu.VMEM((2, 2, 2 * SLICE, BLOCK), BF16)] * 2,
        compiler_params=pltpu.CompilerParams(vmem_limit_bytes=24 * 1024 * 1024),
        cost_estimate=pl.CostEstimate(
            flops=cells * BLOCK * BLOCK * 500, bytes_accessed=1 << 21, transcendentals=cells * BLOCK * BLOCK
        ),
        name=name,
    )(*operands)


def incidence_kernel(corner_ref, out_ref):
    verts, faces = out_ref.shape
    vertex = lax.broadcasted_iota(jnp.int32, (verts, 128), 0)
    for e in range(0, faces, 128):
        total = jnp.zeros((verts, 128), F32)
        for k in range(3):
            total = total + jnp.where(corner_ref[k : k + 1, e : e + 128] == vertex, 1.0, 0.0)
        out_ref[:, e : e + 128] = total.astype(BF16)


def incidence_table(corner, verts):
    faces = corner.shape[1]
    return pl.pallas_call(
        incidence_kernel,
        out_shape=jax.ShapeDtypeStruct((verts, faces), BF16),
        in_specs=[VMEM],
        out_specs=VMEM,
        compiler_params=pltpu.CompilerParams(vmem_limit_bytes=16 * 1024 * 1024),
        cost_estimate=pl.CostEstimate(flops=verts * faces * 9, bytes_accessed=verts * faces * 2, transcendentals=0),
        name="incidence",
    )(corner)


def finish_kernel(parts_ref, table_ref, vertex_ref, face_ref):
    sums = []
    for core in range(2):
        total = parts_ref[core]
        for i in range(core + 2, parts_ref.shape[0], 2):
            total = total + parts_ref[i]
        sums.append(total)
    low, high = sums[1], sums[0]
    total = jnp.concatenate([low[:, :BLOCK], low[:, BLOCK:], high[:, BLOCK:], high[:, :BLOCK]], axis=1)
    faces = total.shape[1]
    width = 2 * HALO_FACES
    face_ref[...] = total[3:7]
    edges = low[7:8] + high[7:8]
    edge = jnp.concatenate([edges[:, c * width : (c + 1) * width] for c in range(3)], axis=0)
    contract = (((1,), (1,)), ((), ()))
    main = jnp.concatenate(thirds(total[0:3]), axis=0).astype(BF16)
    side = jnp.concatenate(thirds(edge), axis=0).astype(BF16)
    out = lax.dot_general(main, table_ref[:, 0:faces], contract, preferred_element_type=F32)
    out = out + lax.dot_general(side, table_ref[:, faces:], contract, preferred_element_type=F32)
    vertex_ref[...] = (out[0:3] + out[3:6] + out[6:9]) / 3.0


def finish(parts, table):
    verts, faces = table.shape[0], 2 * parts.shape[2]
    return pl.pallas_call(
        finish_kernel,
        out_shape=(jax.ShapeDtypeStruct((3, verts), F32), jax.ShapeDtypeStruct((4, faces), F32)),
        in_specs=[VMEM, VMEM],
        out_specs=(VMEM, VMEM),
        compiler_params=pltpu.CompilerParams(vmem_limit_bytes=16 * 1024 * 1024),
        name="finish",
    )(parts, table)


def shards(centroids, normals, areas, cotangent, pair_code, corner_vertex):
    count, shares = lax.axis_size("blk"), lax.axis_size("pair")
    faces = centroids.shape[1]
    assert shares // 2 * SLICE == faces
    member = lax.axis_index("pair")
    core, slab = member % 2, member // 2
    other_block = slab * SLICE // BLOCK

    place = jnp.stack([core, other_block, slab]).reshape(1, 3)
    codes = pair_code.transpose(0, 1, 3, 2).reshape(1, count)
    own, chunks = prepare(place, codes, centroids, normals, areas.reshape(1, faces))
    rows = lax.all_to_all(chunks, "blk", 0, 0)

    held = lax.all_to_all(pack_codes(codes, rows, shares), "pair", 0, 0)
    counts = tally(place, held)
    scale = cotangent.reshape(1, 1)
    corner = jnp.concatenate(
        [corner_vertex[:, HALO_FACES:-HALO_FACES], corner_vertex[:, :HALO_FACES], corner_vertex[:, -HALO_FACES:]], axis=1
    )
    table = incidence_table(corner, faces // 2)

    block = jax.ShapeDtypeStruct((8, BLOCK), F32)
    edge_row = jax.ShapeDtypeStruct((1, 2 * BLOCK), F32)
    operands = (place, counts, scale, own, rows, *features(place, own, rows))
    outer, edge = pair_call(outer_kernel, (block, edge_row), operands, "outer_block")

    def neighbour(b, member):
        return (b + (1 if member % 2 == 0 else count - 1)) % count * shares + member

    hops = [(b * shares + m, neighbour(b, m)) for b in range(count) for m in range(shares)]
    halo = lax.ppermute(edge, ("blk", "pair"), hops)
    inner = pair_call(inner_kernel, block, operands, "inner_block")
    part = jnp.concatenate([jnp.concatenate([outer, inner], axis=1)[:7], halo], axis=0)
    parts = lax.all_gather(part, "pair")
    return finish(parts, table)


def solution(mesh):
    placed = (
        P(None, "blk"),
        P(None, "blk"),
        P("blk"),
        P(),
        P("blk", "pair", None, None),
        P(None, "blk"),
    )
    return jax.shard_map(
        shards,
        mesh=mesh,
        in_specs=placed,
        out_specs=(P(None, "blk"), P(None, "blk")),
        check_vma=False,
    )
```

```python
import functools

import jax
import jax.numpy as jnp
from jax import lax
from jax.experimental import pallas as pl
from jax.experimental.pallas import tpu as pltpu
from jax.sharding import PartitionSpec as P

BLOCK = 256
FB_DEV = 4
HALO_FACES = 64
CODES = FB_DEV * FB_DEV
DEPTH = 64
SLICE = 128
LEFT = (0, 0, 1, 1, 0, 2)
RIGHT = (0, 1, 0, 1, 2, 0)
ONES = (0, 1, 4)
F32 = jnp.float32
BF16 = jnp.bfloat16
VMEM = pl.BlockSpec(memory_space=pltpu.VMEM)
SMEM = pl.BlockSpec(memory_space=pltpu.SMEM)
dot = functools.partial(jnp.dot, preferred_element_type=F32)


def thirds(values):
    high = values.astype(BF16).astype(F32)
    rest = values - high
    middle = rest.astype(BF16).astype(F32)
    return [high, middle, (rest - middle).astype(BF16).astype(F32)]


def square(x):
    return jnp.sum(x[0:3] * x[0:3], axis=0, keepdims=True)


def lever(x):
    return jnp.sum(x[0:3] * x[3:6], axis=0, keepdims=True)


def partner_features(rows, left_ref, feat_ref, base):
    x = jnp.concatenate(rows, axis=1)
    width = x.shape[1]
    row = lax.broadcasted_iota(jnp.int32, x.shape, 0)
    area = x[6:7]
    x = jnp.where(row >= 6, 1.0, x)
    split = thirds(x)
    extra = thirds(square(x)) + thirds(lever(x)) + [jnp.zeros((10, width), F32)]
    left = jnp.concatenate([split[i] for i in LEFT] + extra, axis=0).astype(BF16)
    feat = jnp.concatenate(thirds(x * area) + [jnp.zeros((8, width), F32)], axis=0).astype(BF16)
    for i in range(len(rows)):
        columns = slice(i * SLICE, (i + 1) * SLICE)
        left_ref[base + i] = left[:, columns]
        feat_ref[base + i] = feat[:, columns]


def own_features(x, right_ref, at):
    row = lax.broadcasted_iota(jnp.int32, (8, BLOCK), 0)
    zero = jnp.zeros((8, BLOCK), F32)
    first, second = row < 3, jnp.logical_and(row >= 3, row < 6)
    center = thirds(-2.0 * x)
    swapped = thirds(jnp.concatenate([x[3:6], x[0:3], x[6:8]], axis=0))
    distance, level = thirds(square(x) + 1.0), thirds(lever(x))
    sides = (
        [jnp.where(first, center[i], zero) for i in RIGHT],
        [jnp.where(first, -swapped[i], zero) for i in RIGHT],
        [jnp.where(second, swapped[i], zero) for i in RIGHT],
    )
    for i, g in enumerate(ONES):
        sides[0][g] = jnp.where(row == 7, distance[i], sides[0][g])
        sides[1][g] = jnp.where(row == 7, level[i], sides[1][g])
    tails = (jnp.where(first, 1.0, zero), zero, jnp.where(second, -1.0, zero))
    for m in range(3):
        right_ref[at, m] = jnp.concatenate(sides[m] + [tails[m], zero], axis=0).astype(BF16)


def own_block(core, at):
    return jnp.where(core == 0, FB_DEV - 1 - at, at)


def feature_kernel(place_ref, own_ref, rows_ref, left_ref, feat_ref, right_ref):
    for at in range(2):
        first = pl.multiple_of(own_block(place_ref[0, 0], at) * BLOCK, BLOCK)
        own_features(own_ref[:, pl.ds(first, BLOCK)], right_ref, at)
    for k in range(0, rows_ref.shape[0], 8):
        partner_features([rows_ref[k + i] for i in range(8)], left_ref, feat_ref, k)


def features(place, own, rows):
    n = rows.shape[0]
    return pl.pallas_call(
        feature_kernel,
        out_shape=(
            jax.ShapeDtypeStruct((n, DEPTH, SLICE), BF16),
            jax.ShapeDtypeStruct((n, 32, SLICE), BF16),
            jax.ShapeDtypeStruct((2, 3, DEPTH, BLOCK), BF16),
        ),
        in_specs=[SMEM, VMEM, VMEM],
        out_specs=(VMEM, VMEM, VMEM),
        compiler_params=pltpu.CompilerParams(vmem_limit_bytes=16 * 1024 * 1024),
        cost_estimate=pl.CostEstimate(flops=1 << 22, bytes_accessed=1 << 20, transcendentals=0),
        name="features",
    )(place, own, rows)


def tally_kernel(place_ref, held_ref, out_ref):
    other = place_ref[0, 1]
    held = held_ref[...]
    lanes = held.shape[2]
    half = lanes // 2
    lane = lax.broadcasted_iota(jnp.int32, (1, lanes), 1)
    rows = []
    for o in range(FB_DEV):
        code = jnp.where(lane < half, o * FB_DEV + other, other * FB_DEV + o)
        rows.append(jnp.sum(jnp.where(held == code[None], 1.0, 0.0), axis=0))
    counts = jnp.concatenate(rows + [jnp.zeros((8 - FB_DEV, lanes), F32)], axis=0).T
    active = counts > 0.0
    at, before = (lax.broadcasted_iota(jnp.int32, (lanes, lanes), i) for i in range(2))
    upto = jnp.logical_and(before <= at, (before < half) == (at < half))
    order = dot(jnp.where(upto, 1.0, 0.0).astype(BF16), jnp.where(active, 1.0, 0.0).astype(BF16)).astype(jnp.int32)
    place = jnp.where(active, order - 1, -1)
    index = lax.broadcasted_iota(jnp.int32, counts.shape, 0) % half
    value = counts.astype(jnp.int32) * 256 + index
    slot = lax.broadcasted_iota(jnp.int32, (half, 128), 1)
    for o in range(FB_DEV):
        for role in range(2):
            mine = slice(role * half, (role + 1) * half)
            hit = slot == place[mine, o : o + 1]
            entries = jnp.sum(jnp.where(hit, value[mine, o : o + 1].astype(F32), 0.0), axis=0, keepdims=True)
            total = order[(role + 1) * half - 1 : (role + 1) * half, o : o + 1].astype(F32)
            entries = jnp.where(slot[0:1] == 127, total, entries)
            out_ref[o : o + 1, role * 128 : (role + 1) * 128] = entries.astype(jnp.int32)


def tally(place, held):
    return pl.pallas_call(
        tally_kernel,
        out_shape=jax.ShapeDtypeStruct((FB_DEV, 256), jnp.int32),
        in_specs=[SMEM, VMEM],
        out_specs=VMEM,
        compiler_params=pltpu.CompilerParams(vmem_limit_bytes=16 * 1024 * 1024),
        name="tally",
    )(place, held)


def prepare_kernel(place_ref, code_ref, center_ref, normal_ref, area_ref, row_ref, own_ref, chunk_ref):
    own_ref[0:3, :] = center_ref[...]
    own_ref[3:6, :] = normal_ref[...]
    own_ref[6:7, :] = area_ref[...]
    own_ref[7:8, :] = jnp.zeros_like(area_ref)
    own_ref[7:8, : row_ref.shape[1]] = row_ref[...].astype(F32)
    piece = own_ref[:, pl.ds(pl.multiple_of(place_ref[0, 2] * SLICE, SLICE), SLICE)]
    last = lax.broadcasted_iota(jnp.int32, piece.shape, 0) == 7
    for b in range(chunk_ref.shape[0]):
        chunk_ref[b] = jnp.where(last, code_ref[0, b].astype(F32), piece)


def prepare(place, codes, centroids, normals, areas):
    count, faces = codes.shape[1], centroids.shape[1]
    return pl.pallas_call(
        prepare_kernel,
        out_shape=(jax.ShapeDtypeStruct((8, faces), F32), jax.ShapeDtypeStruct((count, 8, SLICE), F32)),
        in_specs=[SMEM, SMEM, VMEM, VMEM, VMEM, VMEM],
        out_specs=(VMEM, VMEM),
        compiler_params=pltpu.CompilerParams(vmem_limit_bytes=60 * 1024 * 1024),
        name="prepare",
    )(place, codes, centroids, normals, areas, codes)


def pack_kernel(own_ref, rows_ref, out_ref):
    values = rows_ref[:, 7, :]
    count = values.shape[0]
    lane, row = (lax.broadcasted_iota(jnp.int32, values.shape, i) for i in (1, 0))
    incoming = jnp.sum(jnp.where(lane == row, values, 0.0), axis=0, keepdims=True)
    both_ways = jnp.concatenate([incoming[:, :count], own_ref[7:8, :count]], axis=1).astype(jnp.int32)
    out_ref[...] = jnp.broadcast_to(both_ways[None], out_ref.shape)


def pack_codes(own, rows, shares):
    return pl.pallas_call(
        pack_kernel,
        out_shape=jax.ShapeDtypeStruct((shares, 1, 2 * rows.shape[0]), jnp.int32),
        in_specs=[VMEM, VMEM],
        out_specs=VMEM,
        compiler_params=pltpu.CompilerParams(vmem_limit_bytes=16 * 1024 * 1024),
        name="pack_codes",
    )(own, rows)


class Steps:
    def __init__(self, mine, list_ref):
        self.mine, self.list_ref = mine, list_ref
        self.first = (list_ref[mine, 127] + 1) // 2
        self.number = self.first + (list_ref[mine, 255] + 1) // 2

    def role(self, step):
        return (step >= self.first).astype(jnp.int32)

    def entry(self, step, h):
        role = self.role(step)
        entry = self.list_ref[self.mine, role * 128 + 2 * (step - role * self.first) + h]
        return entry // 256, entry % 256

    def beside(self, step, ref):
        return jnp.concatenate([ref[self.entry(step, h)[1]] for h in range(2)], axis=1)


def products(step, steps, left_ref, right_ref, at, out_ref):
    left = steps.beside(step, left_ref)
    over = (((0,), (0,)), ((), ()))
    out_ref[0] = lax.dot_general(left, right_ref[at, 0], over, preferred_element_type=F32)
    out_ref[1] = lax.dot_general(left, right_ref[at, 1 + steps.role(step)], over, preferred_element_type=F32)


def weights(step, steps, rows_ref, in_ref, out_ref, kernel_ref):
    for h in range(2):
        count, x = steps.entry(step, h)
        area = rows_ref[x].T[:, 6:7]
        here = slice(h * SLICE, (h + 1) * SLICE)
        inverse = pl.reciprocal(in_ref[0, here], approx=True)
        projected = in_ref[1, here]
        scaled = inverse * inverse * count.astype(F32)
        kernel = (projected * projected + 1.0) * scaled
        kernel_ref[...] += jnp.sum((kernel * area).reshape(SLICE // 8, 8, BLOCK), axis=0)
        for m, values in enumerate((kernel * inverse, projected * scaled)):
            high = values.astype(BF16)
            out_ref[m, 0, here] = high
            out_ref[m, 1, here] = (values - high.astype(F32)).astype(BF16)


def reduce_cells(step, steps, feat_ref, in_ref, acc_ref):
    feat = steps.beside(step, feat_ref)
    for m, place in enumerate((0, 1 + steps.role(step))):
        acc_ref[place] += dot(feat, in_ref[m, 0]) + dot(feat, in_ref[m, 1])


def pair_body(at, place_ref, list_ref, scale_ref, own_ref, rows_ref, left_ref, feat_ref, right_ref, out_ref, acc_ref, kernel_ref, *stages):
    product_refs, weight_refs = stages[:2], stages[2:]
    mine = own_block(place_ref[0, 0], at)
    steps = Steps(mine, list_ref)
    own = own_ref[:, pl.ds(pl.multiple_of(mine * BLOCK, BLOCK), BLOCK)]
    acc_ref[...] = jnp.zeros_like(acc_ref)
    kernel_ref[...] = jnp.zeros_like(kernel_ref)
    weight_refs[1][...] = jnp.zeros_like(weight_refs[1])
    products(0, steps, left_ref, right_ref, at, product_refs[0])

    def visit(i, carry):
        for u in range(2):
            now, later, step = u, 1 - u, 2 * i + u
            reduce_cells(jnp.maximum(step - 1, 0), steps, feat_ref, weight_refs[later], acc_ref)
            weights(step, steps, rows_ref, product_refs[now], weight_refs[now], kernel_ref)
            products(step + 1, steps, left_ref, right_ref, at, product_refs[later])
        return carry

    rounds = (steps.number + 1) // 2
    lax.fori_loop(0, rounds, visit, 0)
    reduce_cells(jnp.maximum(2 * rounds - 1, 0), steps, feat_ref, weight_refs[1], acc_ref)

    scale = scale_ref[0, 0]
    pushing, target, source = (acc_ref[m, 0:8] + acc_ref[m, 8:16] + acc_ref[m, 16:24] for m in range(3))
    center, normal = own[0:3], own[3:6]
    weight = scale * own[6:7]
    push = center * pushing[6:7] - pushing[0:3]
    pull = normal * target[6:7] + source[3:6]
    out_ref[0:3, :] = weight * (2.0 * pull - 4.0 * push)
    out_ref[3:6, :] = 2.0 * weight * (center * target[6:7] - target[0:3])
    out_ref[6:7, :] = scale * jnp.sum(kernel_ref[...], axis=0, keepdims=True)
    out_ref[7:8, :] = jnp.zeros((1, BLOCK), F32)


def outer_kernel(*refs):
    place_ref, (out_ref, edge_ref), scratch = refs[0], refs[8:10], refs[10:]
    pair_body(0, *refs[:8], out_ref, *scratch)
    core = place_ref[0, 0]
    gap = jnp.zeros((1, HALO_FACES), F32)
    tails, heads = [], []
    for c in range(3):
        tails += [out_ref[c : c + 1, BLOCK - HALO_FACES :], gap]
        heads += [gap, out_ref[c : c + 1, :HALO_FACES]]
    rest = [gap] * (2 * BLOCK // HALO_FACES - 6)
    edge_ref[...] = jnp.where(core == 0, jnp.concatenate(tails + rest, axis=1), jnp.concatenate(heads + rest, axis=1))


def inner_kernel(*refs):
    pair_body(1, *refs)


def pair_call(body, outputs, operands, name):
    cells = operands[4].shape[0] // 3
    in_specs = [SMEM] * 3 + [VMEM] * (len(operands) - 3)
    return pl.pallas_call(
        body,
        out_shape=outputs,
        in_specs=in_specs,
        out_specs=jax.tree.map(lambda _: VMEM, outputs),
        scratch_shapes=[
            pltpu.VMEM((3, 32, BLOCK), F32),
            pltpu.VMEM((8, BLOCK), F32),
        ]
        + [pltpu.VMEM((2, 2 * SLICE, BLOCK), F32)] * 2
        + [pltpu.VMEM((2, 2, 2 * SLICE, BLOCK), BF16)] * 2,
        compiler_params=pltpu.CompilerParams(vmem_limit_bytes=24 * 1024 * 1024),
        cost_estimate=pl.CostEstimate(
            flops=cells * BLOCK * BLOCK * 500, bytes_accessed=1 << 21, transcendentals=cells * BLOCK * BLOCK
        ),
        name=name,
    )(*operands)


def incidence_kernel(corner_ref, out_ref):
    verts, faces = out_ref.shape
    vertex = lax.broadcasted_iota(jnp.int32, (verts, 128), 0)
    window = corner_ref[...]
    inside, ends = window[:, HALO_FACES:-HALO_FACES], (window[:, :HALO_FACES], window[:, -HALO_FACES:])
    corner = jnp.concatenate([inside, *ends], axis=1)
    for e in range(0, faces, 128):
        total = jnp.zeros((verts, 128), F32)
        for k in range(3):
            total = total + jnp.where(corner[k : k + 1, e : e + 128] == vertex, 1.0, 0.0)
        out_ref[:, e : e + 128] = total.astype(BF16)


def incidence_table(corner, verts):
    faces = corner.shape[1]
    return pl.pallas_call(
        incidence_kernel,
        out_shape=jax.ShapeDtypeStruct((verts, faces), BF16),
        in_specs=[VMEM],
        out_specs=VMEM,
        compiler_params=pltpu.CompilerParams(vmem_limit_bytes=16 * 1024 * 1024),
        cost_estimate=pl.CostEstimate(flops=verts * faces * 9, bytes_accessed=verts * faces * 2, transcendentals=0),
        name="incidence",
    )(corner)


def finish_kernel(parts_ref, table_ref, vertex_ref, face_ref):
    sums = []
    for core in range(2):
        total = parts_ref[core]
        for i in range(core + 2, parts_ref.shape[0], 2):
            total = total + parts_ref[i]
        sums.append(total)
    low, high = sums[1], sums[0]
    total = jnp.concatenate([low[:, :BLOCK], low[:, BLOCK:], high[:, BLOCK:], high[:, :BLOCK]], axis=1)
    faces = total.shape[1]
    width = 2 * HALO_FACES
    face_ref[...] = total[3:7]
    edges = low[7:8] + high[7:8]
    edge = jnp.concatenate([edges[:, c * width : (c + 1) * width] for c in range(3)], axis=0)
    contract = (((1,), (1,)), ((), ()))
    main = jnp.concatenate(thirds(total[0:3]), axis=0).astype(BF16)
    side = jnp.concatenate(thirds(edge), axis=0).astype(BF16)
    out = lax.dot_general(main, table_ref[:, 0:faces], contract, preferred_element_type=F32)
    out = out + lax.dot_general(side, table_ref[:, faces:], contract, preferred_element_type=F32)
    vertex_ref[...] = (out[0:3] + out[3:6] + out[6:9]) / 3.0


def finish(parts, table):
    verts, faces = table.shape[0], 2 * parts.shape[2]
    return pl.pallas_call(
        finish_kernel,
        out_shape=(jax.ShapeDtypeStruct((3, verts), F32), jax.ShapeDtypeStruct((4, faces), F32)),
        in_specs=[VMEM, VMEM],
        out_specs=(VMEM, VMEM),
        compiler_params=pltpu.CompilerParams(vmem_limit_bytes=16 * 1024 * 1024),
        name="finish",
    )(parts, table)


def shards(centroids, normals, areas, cotangent, pair_code, corner_vertex):
    count, shares = lax.axis_size("blk"), lax.axis_size("pair")
    faces = centroids.shape[1]
    assert shares // 2 * SLICE == faces
    member = lax.axis_index("pair")
    core, slab = member % 2, member // 2
    other_block = slab * SLICE // BLOCK

    place = jnp.stack([core, other_block, slab]).reshape(1, 3)
    codes = pair_code.transpose(0, 1, 3, 2).reshape(1, count)
    own, chunks = prepare(place, codes, centroids, normals, areas.reshape(1, faces))
    rows = lax.all_to_all(chunks, "blk", 0, 0)

    held = lax.all_to_all(pack_codes(own, rows, shares), "pair", 0, 0)
    counts = tally(place, held)
    scale = cotangent.reshape(1, 1)
    table = incidence_table(corner_vertex, faces // 2)

    block = jax.ShapeDtypeStruct((8, BLOCK), F32)
    edge_row = jax.ShapeDtypeStruct((1, 2 * BLOCK), F32)
    operands = (place, counts, scale, own, rows, *features(place, own, rows))
    outer, edge = pair_call(outer_kernel, (block, edge_row), operands, "outer_block")

    def neighbour(b, member):
        return (b + (1 if member % 2 == 0 else count - 1)) % count * shares + member

    hops = [(b * shares + m, neighbour(b, m)) for b in range(count) for m in range(shares)]
    halo = lax.ppermute(edge, ("blk", "pair"), hops)
    inner = pair_call(inner_kernel, block, operands, "inner_block")
    part = jnp.concatenate([jnp.concatenate([outer, inner], axis=1)[:7], halo], axis=0)
    parts = lax.all_gather(part, "pair")
    return finish(parts, table)


def solution(mesh):
    placed = (
        P(None, "blk"),
        P(None, "blk"),
        P("blk"),
        P(),
        P("blk", "pair", None, None),
        P(None, "blk"),
    )
    return jax.shard_map(
        shards,
        mesh=mesh,
        in_specs=placed,
        out_specs=(P(None, "blk"), P(None, "blk")),
        check_vma=False,
    )
```

```python
import functools

import jax
import jax.numpy as jnp
from jax import lax
from jax.experimental import pallas as pl
from jax.experimental.pallas import tpu as pltpu
from jax.sharding import PartitionSpec as P

BLOCK = 256
FB_DEV = 4
HALO_FACES = 64
CODES = FB_DEV * FB_DEV
DEPTH = 64
SLICE = 128
LEFT = (0, 0, 1, 1, 0, 2)
RIGHT = (0, 1, 0, 1, 2, 0)
ONES = (0, 1, 4)
F32 = jnp.float32
BF16 = jnp.bfloat16
VMEM = pl.BlockSpec(memory_space=pltpu.VMEM)
SMEM = pl.BlockSpec(memory_space=pltpu.SMEM)
dot = functools.partial(jnp.dot, preferred_element_type=F32)


def thirds(values):
    high = values.astype(BF16).astype(F32)
    rest = values - high
    middle = rest.astype(BF16).astype(F32)
    return [high, middle, (rest - middle).astype(BF16).astype(F32)]


def square(x):
    return jnp.sum(x[0:3] * x[0:3], axis=0, keepdims=True)


def lever(x):
    return jnp.sum(x[0:3] * x[3:6], axis=0, keepdims=True)


def partner_features(rows, left_ref, feat_ref, base):
    x = jnp.concatenate(rows, axis=1)
    width = x.shape[1]
    row = lax.broadcasted_iota(jnp.int32, x.shape, 0)
    area = x[6:7]
    x = jnp.where(row >= 6, 1.0, x)
    split = thirds(x)
    extra = thirds(square(x)) + thirds(lever(x)) + [jnp.zeros((10, width), F32)]
    left = jnp.concatenate([split[i] for i in LEFT] + extra, axis=0).astype(BF16)
    feat = jnp.concatenate(thirds(x * area) + [jnp.zeros((8, width), F32)], axis=0).astype(BF16)
    for i in range(len(rows)):
        columns = slice(i * SLICE, (i + 1) * SLICE)
        left_ref[base + i] = left[:, columns]
        feat_ref[base + i] = feat[:, columns]


def own_features(x, right_ref, at):
    row = lax.broadcasted_iota(jnp.int32, (8, BLOCK), 0)
    zero = jnp.zeros((8, BLOCK), F32)
    first, second = row < 3, jnp.logical_and(row >= 3, row < 6)
    center = thirds(-2.0 * x)
    swapped = thirds(jnp.concatenate([x[3:6], x[0:3], x[6:8]], axis=0))
    distance, level = thirds(square(x) + 1.0), thirds(lever(x))
    sides = (
        [jnp.where(first, center[i], zero) for i in RIGHT],
        [jnp.where(first, -swapped[i], zero) for i in RIGHT],
        [jnp.where(second, swapped[i], zero) for i in RIGHT],
    )
    for i, g in enumerate(ONES):
        sides[0][g] = jnp.where(row == 7, distance[i], sides[0][g])
        sides[1][g] = jnp.where(row == 7, level[i], sides[1][g])
    tails = (jnp.where(first, 1.0, zero), zero, jnp.where(second, -1.0, zero))
    for m in range(3):
        right_ref[at, m] = jnp.concatenate(sides[m] + [tails[m], zero], axis=0).astype(BF16)


def own_block(core, at):
    return jnp.where(core == 0, FB_DEV - 1 - at, at)


def feature_kernel(place_ref, own_ref, rows_ref, left_ref, feat_ref, right_ref):
    for at in range(2):
        first = pl.multiple_of(own_block(place_ref[0, 0], at) * BLOCK, BLOCK)
        own_features(own_ref[:, pl.ds(first, BLOCK)], right_ref, at)
    for k in range(0, rows_ref.shape[0], 8):
        partner_features([rows_ref[k + i] for i in range(8)], left_ref, feat_ref, k)


def features(place, own, rows):
    n = rows.shape[0]
    return pl.pallas_call(
        feature_kernel,
        out_shape=(
            jax.ShapeDtypeStruct((n, DEPTH, SLICE), BF16),
            jax.ShapeDtypeStruct((n, 32, SLICE), BF16),
            jax.ShapeDtypeStruct((2, 3, DEPTH, BLOCK), BF16),
        ),
        in_specs=[SMEM, VMEM, VMEM],
        out_specs=(VMEM, VMEM, VMEM),
        compiler_params=pltpu.CompilerParams(vmem_limit_bytes=16 * 1024 * 1024),
        cost_estimate=pl.CostEstimate(flops=1 << 22, bytes_accessed=1 << 20, transcendentals=0),
        name="features",
    )(place, own, rows)


def tally_kernel(place_ref, held_ref, out_ref):
    other = place_ref[0, 1]
    held = held_ref[...]
    lanes = held.shape[2]
    half = lanes // 2
    lane = lax.broadcasted_iota(jnp.int32, (1, lanes), 1)
    rows = []
    for o in range(FB_DEV):
        code = jnp.where(lane < half, o * FB_DEV + other, other * FB_DEV + o)
        rows.append(jnp.sum(jnp.where(held == code[None], 1.0, 0.0), axis=0))
    counts = jnp.concatenate(rows + [jnp.zeros((8 - FB_DEV, lanes), F32)], axis=0).T
    active = counts > 0.0
    at, before = (lax.broadcasted_iota(jnp.int32, (lanes, lanes), i) for i in range(2))
    upto = jnp.logical_and(before <= at, (before < half) == (at < half))
    order = dot(jnp.where(upto, 1.0, 0.0).astype(BF16), jnp.where(active, 1.0, 0.0).astype(BF16)).astype(jnp.int32)
    place = jnp.where(active, order - 1, -1)
    index = lax.broadcasted_iota(jnp.int32, counts.shape, 0) % half
    value = counts.astype(jnp.int32) * 256 + index
    slot = lax.broadcasted_iota(jnp.int32, (half, 128), 1)
    for o in range(FB_DEV):
        for role in range(2):
            mine = slice(role * half, (role + 1) * half)
            hit = slot == place[mine, o : o + 1]
            entries = jnp.sum(jnp.where(hit, value[mine, o : o + 1].astype(F32), 0.0), axis=0, keepdims=True)
            total = order[(role + 1) * half - 1 : (role + 1) * half, o : o + 1].astype(F32)
            entries = jnp.where(slot[0:1] == 127, total, entries)
            out_ref[o : o + 1, role * 128 : (role + 1) * 128] = entries.astype(jnp.int32)


def tally(place, held):
    return pl.pallas_call(
        tally_kernel,
        out_shape=jax.ShapeDtypeStruct((FB_DEV, 256), jnp.int32),
        in_specs=[SMEM, VMEM],
        out_specs=VMEM,
        compiler_params=pltpu.CompilerParams(vmem_limit_bytes=16 * 1024 * 1024),
        name="tally",
    )(place, held)


def prepare_kernel(code_ref, center_ref, normal_ref, area_ref, row_ref, own_ref, chunk_ref):
    own_ref[0:3, :] = center_ref[...]
    own_ref[3:6, :] = normal_ref[...]
    own_ref[6:7, :] = area_ref[...]
    own_ref[7:8, :] = jnp.zeros_like(area_ref)
    own_ref[7:8, : row_ref.shape[1]] = row_ref[...].astype(F32)
    piece = own_ref[:, pl.ds(pl.multiple_of(lax.axis_index("pair") // 2 * SLICE, SLICE), SLICE)]
    last = lax.broadcasted_iota(jnp.int32, piece.shape, 0) == 7
    for b in range(chunk_ref.shape[0]):
        chunk_ref[b] = jnp.where(last, code_ref[0, b].astype(F32), piece)


def prepare(codes, centroids, normals, areas):
    count, faces = codes.shape[1], centroids.shape[1]
    return pl.pallas_call(
        prepare_kernel,
        out_shape=(jax.ShapeDtypeStruct((8, faces), F32), jax.ShapeDtypeStruct((count, 8, SLICE), F32)),
        in_specs=[SMEM, VMEM, VMEM, VMEM, VMEM],
        out_specs=(VMEM, VMEM),
        compiler_params=pltpu.CompilerParams(vmem_limit_bytes=60 * 1024 * 1024),
        name="prepare",
    )(codes, centroids, normals, areas, codes)


def pack_kernel(own_ref, rows_ref, out_ref):
    values = rows_ref[:, 7, :]
    count = values.shape[0]
    lane, row = (lax.broadcasted_iota(jnp.int32, values.shape, i) for i in (1, 0))
    incoming = jnp.sum(jnp.where(lane == row, values, 0.0), axis=0, keepdims=True)
    both_ways = jnp.concatenate([incoming[:, :count], own_ref[7:8, :count]], axis=1).astype(jnp.int32)
    out_ref[...] = jnp.broadcast_to(both_ways[None], out_ref.shape)


def pack_codes(own, rows, shares):
    return pl.pallas_call(
        pack_kernel,
        out_shape=jax.ShapeDtypeStruct((shares, 1, 2 * rows.shape[0]), jnp.int32),
        in_specs=[VMEM, VMEM],
        out_specs=VMEM,
        compiler_params=pltpu.CompilerParams(vmem_limit_bytes=16 * 1024 * 1024),
        name="pack_codes",
    )(own, rows)


class Steps:
    def __init__(self, mine, list_ref):
        self.mine, self.list_ref = mine, list_ref
        self.first = (list_ref[mine, 127] + 1) // 2
        self.number = self.first + (list_ref[mine, 255] + 1) // 2

    def role(self, step):
        return (step >= self.first).astype(jnp.int32)

    def entry(self, step, h):
        role = self.role(step)
        entry = self.list_ref[self.mine, role * 128 + 2 * (step - role * self.first) + h]
        return entry // 256, entry % 256

    def beside(self, step, ref):
        return jnp.concatenate([ref[self.entry(step, h)[1]] for h in range(2)], axis=1)


def products(step, steps, left_ref, right_ref, at, out_ref):
    left = steps.beside(step, left_ref)
    over = (((0,), (0,)), ((), ()))
    out_ref[0] = lax.dot_general(left, right_ref[at, 0], over, preferred_element_type=F32)
    out_ref[1] = lax.dot_general(left, right_ref[at, 1 + steps.role(step)], over, preferred_element_type=F32)


def weights(step, steps, rows_ref, in_ref, out_ref, kernel_ref):
    for h in range(2):
        count, x = steps.entry(step, h)
        area = rows_ref[x].T[:, 6:7]
        here = slice(h * SLICE, (h + 1) * SLICE)
        inverse = pl.reciprocal(in_ref[0, here], approx=True)
        projected = in_ref[1, here]
        scaled = inverse * inverse * count.astype(F32)
        kernel = (projected * projected + 1.0) * scaled
        kernel_ref[...] += jnp.sum((kernel * area).reshape(SLICE // 8, 8, BLOCK), axis=0)
        for m, values in enumerate((kernel * inverse, projected * scaled)):
            high = values.astype(BF16)
            out_ref[m, 0, here] = high
            out_ref[m, 1, here] = (values - high.astype(F32)).astype(BF16)


def reduce_cells(step, steps, feat_ref, in_ref, acc_ref):
    feat = steps.beside(step, feat_ref)
    for m, place in enumerate((0, 1 + steps.role(step))):
        acc_ref[place] += dot(feat, in_ref[m, 0]) + dot(feat, in_ref[m, 1])


def pair_body(at, place_ref, list_ref, scale_ref, own_ref, rows_ref, left_ref, feat_ref, right_ref, out_ref, acc_ref, kernel_ref, *stages):
    product_refs, weight_refs = stages[:2], stages[2:]
    mine = own_block(place_ref[0, 0], at)
    steps = Steps(mine, list_ref)
    own = own_ref[:, pl.ds(pl.multiple_of(mine * BLOCK, BLOCK), BLOCK)]
    acc_ref[...] = jnp.zeros_like(acc_ref)
    kernel_ref[...] = jnp.zeros_like(kernel_ref)
    weight_refs[1][...] = jnp.zeros_like(weight_refs[1])
    products(0, steps, left_ref, right_ref, at, product_refs[0])

    def visit(i, carry):
        for u in range(2):
            now, later, step = u, 1 - u, 2 * i + u
            reduce_cells(jnp.maximum(step - 1, 0), steps, feat_ref, weight_refs[later], acc_ref)
            weights(step, steps, rows_ref, product_refs[now], weight_refs[now], kernel_ref)
            products(step + 1, steps, left_ref, right_ref, at, product_refs[later])
        return carry

    rounds = (steps.number + 1) // 2
    lax.fori_loop(0, rounds, visit, 0)
    reduce_cells(jnp.maximum(2 * rounds - 1, 0), steps, feat_ref, weight_refs[1], acc_ref)

    scale = scale_ref[0, 0]
    pushing, target, source = (acc_ref[m, 0:8] + acc_ref[m, 8:16] + acc_ref[m, 16:24] for m in range(3))
    center, normal = own[0:3], own[3:6]
    weight = scale * own[6:7]
    push = center * pushing[6:7] - pushing[0:3]
    pull = normal * target[6:7] + source[3:6]
    out_ref[0:3, :] = weight * (2.0 * pull - 4.0 * push)
    out_ref[3:6, :] = 2.0 * weight * (center * target[6:7] - target[0:3])
    out_ref[6:7, :] = scale * jnp.sum(kernel_ref[...], axis=0, keepdims=True)
    out_ref[7:8, :] = jnp.zeros((1, BLOCK), F32)


def outer_kernel(*refs):
    place_ref, (out_ref, edge_ref), scratch = refs[0], refs[8:10], refs[10:]
    pair_body(0, *refs[:8], out_ref, *scratch)
    core = place_ref[0, 0]
    gap = jnp.zeros((1, HALO_FACES), F32)
    tails, heads = [], []
    for c in range(3):
        tails += [out_ref[c : c + 1, BLOCK - HALO_FACES :], gap]
        heads += [gap, out_ref[c : c + 1, :HALO_FACES]]
    rest = [gap] * (2 * BLOCK // HALO_FACES - 6)
    edge_ref[...] = jnp.where(core == 0, jnp.concatenate(tails + rest, axis=1), jnp.concatenate(heads + rest, axis=1))


def inner_kernel(*refs):
    pair_body(1, *refs)


def pair_call(body, outputs, operands, name):
    cells = operands[4].shape[0] // 3
    in_specs = [SMEM] * 3 + [VMEM] * (len(operands) - 3)
    return pl.pallas_call(
        body,
        out_shape=outputs,
        in_specs=in_specs,
        out_specs=jax.tree.map(lambda _: VMEM, outputs),
        scratch_shapes=[
            pltpu.VMEM((3, 32, BLOCK), F32),
            pltpu.VMEM((8, BLOCK), F32),
        ]
        + [pltpu.VMEM((2, 2 * SLICE, BLOCK), F32)] * 2
        + [pltpu.VMEM((2, 2, 2 * SLICE, BLOCK), BF16)] * 2,
        compiler_params=pltpu.CompilerParams(vmem_limit_bytes=24 * 1024 * 1024),
        cost_estimate=pl.CostEstimate(
            flops=cells * BLOCK * BLOCK * 500, bytes_accessed=1 << 21, transcendentals=cells * BLOCK * BLOCK
        ),
        name=name,
    )(*operands)


def incidence_kernel(corner_ref, out_ref):
    verts, faces = out_ref.shape
    vertex = lax.broadcasted_iota(jnp.int32, (verts, 128), 0)
    window = corner_ref[...]
    inside, ends = window[:, HALO_FACES:-HALO_FACES], (window[:, :HALO_FACES], window[:, -HALO_FACES:])
    corner = jnp.concatenate([inside, *ends], axis=1)
    for e in range(0, faces, 128):
        total = jnp.zeros((verts, 128), F32)
        for k in range(3):
            total = total + jnp.where(corner[k : k + 1, e : e + 128] == vertex, 1.0, 0.0)
        out_ref[:, e : e + 128] = total.astype(BF16)


def incidence_table(corner, verts):
    faces = corner.shape[1]
    return pl.pallas_call(
        incidence_kernel,
        out_shape=jax.ShapeDtypeStruct((verts, faces), BF16),
        in_specs=[VMEM],
        out_specs=VMEM,
        compiler_params=pltpu.CompilerParams(vmem_limit_bytes=16 * 1024 * 1024),
        cost_estimate=pl.CostEstimate(flops=verts * faces * 9, bytes_accessed=verts * faces * 2, transcendentals=0),
        name="incidence",
    )(corner)


def finish_kernel(parts_ref, table_ref, vertex_ref, face_ref):
    sums = []
    for core in range(2):
        total = parts_ref[core]
        for i in range(core + 2, parts_ref.shape[0], 2):
            total = total + parts_ref[i]
        sums.append(total)
    low, high = sums[1], sums[0]
    total = jnp.concatenate([low[:, :BLOCK], low[:, BLOCK:], high[:, BLOCK:], high[:, :BLOCK]], axis=1)
    faces = total.shape[1]
    width = 2 * HALO_FACES
    face_ref[...] = total[3:7]
    edges = low[7:8] + high[7:8]
    edge = jnp.concatenate([edges[:, c * width : (c + 1) * width] for c in range(3)], axis=0)
    contract = (((1,), (1,)), ((), ()))
    main = jnp.concatenate(thirds(total[0:3]), axis=0).astype(BF16)
    side = jnp.concatenate(thirds(edge), axis=0).astype(BF16)
    out = lax.dot_general(main, table_ref[:, 0:faces], contract, preferred_element_type=F32)
    out = out + lax.dot_general(side, table_ref[:, faces:], contract, preferred_element_type=F32)
    vertex_ref[...] = (out[0:3] + out[3:6] + out[6:9]) / 3.0


def finish(parts, table):
    verts, faces = table.shape[0], 2 * parts.shape[2]
    return pl.pallas_call(
        finish_kernel,
        out_shape=(jax.ShapeDtypeStruct((3, verts), F32), jax.ShapeDtypeStruct((4, faces), F32)),
        in_specs=[VMEM, VMEM],
        out_specs=(VMEM, VMEM),
        compiler_params=pltpu.CompilerParams(vmem_limit_bytes=16 * 1024 * 1024),
        name="finish",
    )(parts, table)


def shards(centroids, normals, areas, cotangent, pair_code, corner_vertex):
    count, shares = lax.axis_size("blk"), lax.axis_size("pair")
    faces = centroids.shape[1]
    assert shares // 2 * SLICE == faces
    member = lax.axis_index("pair")
    core, slab = member % 2, member // 2
    other_block = slab * SLICE // BLOCK

    place = jnp.stack([core, other_block]).reshape(1, 2)
    codes = pair_code.transpose(0, 1, 3, 2).reshape(1, count)
    own, chunks = prepare(codes, centroids, normals, areas.reshape(1, faces))
    rows = lax.all_to_all(chunks, "blk", 0, 0)

    held = lax.all_to_all(pack_codes(own, rows, shares), "pair", 0, 0)
    counts = tally(place, held)
    scale = cotangent.reshape(1, 1)
    table = incidence_table(corner_vertex, faces // 2)

    block = jax.ShapeDtypeStruct((8, BLOCK), F32)
    edge_row = jax.ShapeDtypeStruct((1, 2 * BLOCK), F32)
    operands = (place, counts, scale, own, rows, *features(place, own, rows))
    outer, edge = pair_call(outer_kernel, (block, edge_row), operands, "outer_block")

    def neighbour(b, member):
        return (b + (1 if member % 2 == 0 else count - 1)) % count * shares + member

    hops = [(b * shares + m, neighbour(b, m)) for b in range(count) for m in range(shares)]
    halo = lax.ppermute(edge, ("blk", "pair"), hops)
    inner = pair_call(inner_kernel, block, operands, "inner_block")
    part = jnp.concatenate([jnp.concatenate([outer, inner], axis=1)[:7], halo], axis=0)
    parts = lax.all_gather(part, "pair")
    return finish(parts, table)


def solution(mesh):
    placed = (
        P(None, "blk"),
        P(None, "blk"),
        P("blk"),
        P(),
        P("blk", "pair", None, None),
        P(None, "blk"),
    )
    return jax.shard_map(
        shards,
        mesh=mesh,
        in_specs=placed,
        out_specs=(P(None, "blk"), P(None, "blk")),
        check_vma=False,
    )
```
